256 devices in a mesh: dp: 32 (over x, z), codebook: 8 (over y, core).
Axes of the slice: x: 4, y: 4, z: 8, core: 2. Of those that a mesh axis runs over, the one named last changes fastest.
Arguments:
- keys: bfloat16 [32768, 128], P('dp'), may hold values from -25 to 25
- codebook: bfloat16 [65536, 128], P(('dp', 'codebook')), may hold values from -6 to 6
Outputs:
- new_codebook: bfloat16 [65536, 128], P(('dp', 'codebook'))
- loglik: float32 [32768], P('dp')
The draws below stay inside these ranges and needn't reach their ends.
All inputs are finite; a program needn't handle non-finite values.
Results may differ from the reference program's by a relative error of at most 0.008.
Values may be sent and summed in bfloat16 or wider, within the bound.
A program may use at most 64 MiB of HBM per device.

```python
import jax
import jax.numpy as jnp
from jax import lax

E = 128
CODE_DEV = 256
ENTRIES = 65536
TOKENS = 32768
N_CODEBOOK = 8


def common_codebook(key, slope):
    base = jnp.clip(jax.random.normal(key, (ENTRIES, E), jnp.float32), -5.5, 5.5)
    rows = jnp.arange(ENTRIES)
    column = (rows // CODE_DEV % N_CODEBOOK).astype(jnp.float32)
    level = column / max(N_CODEBOOK - 1, 1)
    factor = jnp.sqrt(1.0 - slope * level)
    return base * factor[:, None]


def draw_codebook(key, part):
    return common_codebook(key, 14.0 / E).astype(jnp.bfloat16)


def draw_keys(key, part):
    key = jax.random.fold_in(key, 7)
    first = jax.random.fold_in(key, 0)
    base = jnp.clip(jax.random.normal(first, (TOKENS, E), jnp.float32), -5.5, 5.5)
    return base.astype(jnp.bfloat16)


def setup_inputs(seed: int = 0) -> dict:
    key_list = jax.random.split(jax.random.key(seed), 3)
    return {
        "keys": draw_keys(jax.random.fold_in(key_list[2], 71), 0),
        "codebook": draw_codebook(jax.random.fold_in(key_list[2], 71), 0),
    }


BETA = 0.1


def scores_of(keys, sq_key, block):
    cross = jnp.dot(keys, block.T, preferred_element_type=jnp.float32)
    block_f = block.astype(jnp.float32)
    sq_code = jnp.sum(block_f * block_f, axis=1)
    return BETA * (2.0 * cross - sq_key[:, None] - sq_code[None, :])


def reference(keys, codebook):
    keys_f = keys.astype(jnp.float32)
    sq_key = jnp.sum(keys_f * keys_f, axis=1)
    width = min(2048, ENTRIES)
    blocks = codebook.reshape(ENTRIES // width, width, E)

    def online(carry, block):
        peak, total = carry
        score = scores_of(keys, sq_key, block)
        upper = jnp.maximum(peak, jnp.max(score, axis=1))
        total = total * jnp.exp(peak - upper) + jnp.sum(jnp.exp(score - upper[:, None]), axis=1)
        return (upper, total), None

    start = (jnp.full((TOKENS,), -jnp.inf, jnp.float32), jnp.zeros((TOKENS,), jnp.float32))
    (peak, total), unused = lax.scan(online, start, blocks)
    loglik = peak + jnp.log(total)

    def accumulate(block):
        score = scores_of(keys, sq_key, block)
        resp = jnp.exp(score - loglik[:, None]).astype(jnp.bfloat16)
        weighted = jnp.dot(resp.T, keys, preferred_element_type=jnp.float32)
        mass = jnp.sum(resp.astype(jnp.float32), axis=0)
        return weighted, mass

    weighted, mass = lax.map(accumulate, blocks)
    weighted = weighted.reshape(ENTRIES, E)
    mass = mass.reshape(ENTRIES)
    new_codebook = ((weighted + codebook.astype(jnp.float32)) / (mass + 1.0)[:, None]).astype(jnp.bfloat16)
    return new_codebook, loglik
```

```python
import jax
import jax.numpy as jnp
from jax import lax
from jax.experimental import pallas as pl
from jax.experimental.pallas import tpu as pltpu
from jax.sharding import PartitionSpec as P

MESH = pl.DeviceIdType.MESH
NX, NZ, NY = 4, 8, 4
TOK, OWN, E = 1024, 256, 128
TILE = 256
BETA = 0.1
LOG2E = 1.4426950408889634
LN2 = 0.6931471805599453
ALPHA = 2.0 * BETA * LOG2E
NT = (((1,), (1,)), ((), ()))


def ring_order(o, n):
    k = (o + 1) // 2
    odd = o % 2
    return (odd * k + (1 - odd) * (n - k)) % n


def to_tile(row):
    return jnp.concatenate([row[:, 128 * r : 128 * (r + 1)] for r in range(8)], axis=0)


def to_row(tile):
    return jnp.concatenate([tile[r : r + 1, :] for r in range(8)], axis=1)


def kernel(
    keys, code, new_code, loglik,
    kt, cb, aug, prob, top, tot, scale, kst, stats, acc, wsend, wrecv,
    key_send, key_recv, core_send, core_recv, code_send, code_recv,
    stat_send, stat_recv, sum_send, sum_recv,
):
    dp, col = lax.axis_index("dp"), lax.axis_index("codebook")
    x, z = dp // NZ, dp % NZ
    y, core = col // 2, col % 2

    def at(dx=0, dz=0, dy=0, dc=0):
        return (
            lax.rem(x + dx, NX) * NZ + lax.rem(z + dz, NZ),
            lax.rem(y + dy, NY) * 2 + lax.rem(core + dc, 2),
        )

    def plane(r):
        return at(dx=r // 8, dy=(r // 2) % 4, dc=r % 2)

    barrier = pltpu.get_barrier_semaphore()

    def greet_plane(r, carry):
        pl.semaphore_signal(barrier, inc=1, device_id=plane(r), device_id_type=MESH)
        return carry

    def greet_ring(d, carry):
        pl.semaphore_signal(barrier, inc=1, device_id=at(dz=d), device_id_type=MESH)
        return carry

    lax.fori_loop(1, 32, greet_plane, 0)
    lax.fori_loop(1, NZ, greet_ring, 0)

    cb[0] = code[...]
    kt[0, :E, :] = keys[...].astype(jnp.float32).T.astype(jnp.bfloat16)
    row = lax.broadcasted_iota(jnp.int32, (E, TOK), 0)
    ones = jnp.where(row < 3, 1.0, 0.0).astype(jnp.bfloat16)
    for i in range(NX):
        kt[i, E:, :] = ones
    kst[:, E:, :] = jnp.zeros((2, E, TOK), jnp.bfloat16)
    half = pl.ds(pl.multiple_of(core * (E // 2), E // 2), E // 2)

    pl.semaphore_wait(barrier, 31 + NZ - 1)

    def key_copy(p):
        to = (NX - ring_order(p, NX)) % NX
        return pltpu.make_async_remote_copy(
            src_ref=kt.at[0, half], dst_ref=kt.at[p, half],
            send_sem=key_send.at[p], recv_sem=key_recv.at[p],
            device_id=at(dx=to), device_id_type=MESH,
        )

    def code_copy(o):
        to = (NZ - ring_order(o, NZ)) % NZ
        return pltpu.make_async_remote_copy(
            src_ref=code, dst_ref=cb.at[o],
            send_sem=code_send.at[o], recv_sem=code_recv.at[o],
            device_id=at(dz=to), device_id_type=MESH,
        )

    def core_copy(p):
        return pltpu.make_async_remote_copy(
            src_ref=kt.at[p, half], dst_ref=kt.at[p, half],
            send_sem=core_send.at[p], recv_sem=core_recv.at[p],
            device_id=at(dc=1), device_id_type=MESH,
        )

    for p in range(1, NX):
        key_copy(p).start()
    for o in range(1, NZ):
        code_copy(o).start()

    def prepare(o):
        c = cb[o].astype(jnp.float32)
        h = -0.5 * jnp.sum(c * c, axis=1, keepdims=True)
        hi = h.astype(jnp.bfloat16).astype(jnp.float32)
        mid = (h - hi).astype(jnp.bfloat16).astype(jnp.float32)
        lo = h - hi - mid
        lane = lax.broadcasted_iota(jnp.int32, (OWN, E), 1)
        both = jnp.where(lane == 0, hi, jnp.where(lane == 1, mid, lo))
        aug[o] = jnp.where(lane < 3, both, 0.0).astype(jnp.bfloat16)

    def unit(i, o):
        c = jnp.concatenate([cb[o], aug[o]], axis=1)
        n = TOK // TILE

        def cross(q):
            k = kt[i, :, q * TILE : (q + 1) * TILE]
            return jnp.dot(c, k, preferred_element_type=jnp.float32)

        s = cross(0)
        for q in range(n):
            later = cross(q + 1) if q + 1 < n else None
            m = jnp.max(s, axis=0, keepdims=True)
            p = jnp.exp2((s - m) * ALPHA)
            span = slice(q * TILE, (q + 1) * TILE)
            top[i, pl.ds(o, 1), span] = m
            tot[i, pl.ds(o, 1), span] = jnp.sum(p, axis=0, keepdims=True)
            prob[i * NZ + o, :, span] = p.astype(jnp.bfloat16)
            s = later

    def arrive(o):
        code_copy(o).wait_recv()
        prepare(o)

    def first(o, carry):
        @pl.when(o > 0)
        def _():
            arrive(o)

        unit(0, o)
        return carry

    def near(n, carry):
        unit(1 + n // 5, n % 5)
        return carry

    def far(n, carry):
        @pl.when(n % 3 == 0)
        def _():
            arrive(5 + n // 3)

        unit(n % 3, 5 + n // 3)
        return carry

    def last(o, carry):
        unit(3, o)
        return carry

    def stat_copy(i, r):
        away = (ring_order(i, NX) + NX - r // 8) % NX
        slot = away + away // 2 - 2 * (away // 3)
        return pltpu.make_async_remote_copy(
            src_ref=stats.at[i, 0], dst_ref=stats.at[slot, r],
            send_sem=stat_send.at[i], recv_sem=stat_recv.at[slot],
            device_id=plane(r), device_id_type=MESH,
        )

    def local_sum(i):
        m = top[i]
        peak = jnp.max(m, axis=0, keepdims=True)
        total = jnp.sum(tot[i] * jnp.exp2((m - peak) * ALPHA), axis=0, keepdims=True)
        stats[i, 0] = to_tile(ALPHA * peak + jnp.log2(total))

    def send_stats(i):
        local_sum(i)

        def go(r, carry):
            stat_copy(i, r).start()
            return carry

        lax.fori_loop(1, 32, go, 0)

    def all_stats(i):
        return pltpu.make_async_remote_copy(
            src_ref=stats.at[i, pl.ds(1, 31)], dst_ref=stats.at[i, pl.ds(1, 31)],
            send_sem=stat_send.at[i], recv_sem=stat_recv.at[i],
            device_id=at(dc=1), device_id_type=MESH,
        )

    def finish_stats(i):
        all_stats(i).wait_recv()
        v = stats[i]
        peak = jnp.max(v, axis=0)
        lse = peak + jnp.log2(jnp.sum(jnp.exp2(v - peak[None]), axis=0))
        if i == 0:
            k = kt[0, :E, :].astype(jnp.float32)
            sq = to_tile(jnp.sum(k * k, axis=0, keepdims=True))
            loglik[...] = LN2 * lse - BETA * sq
        scale[i] = jnp.exp2(ALPHA * top[i] - to_row(lse))

    def weigh(i, o):
        f = scale[i, pl.ds(o, 1), :]
        b = i % 2
        kst[b, :E, :] = (kt[i, :E, :].astype(jnp.float32) * f).astype(jnp.bfloat16)
        sub = lax.broadcasted_iota(jnp.int32, (16, TOK), 0)
        kst[b, E : E + 16, :] = jnp.where(sub == 0, f, 0.0).astype(jnp.bfloat16)
        return lax.dot_general(prob[i * NZ + o], kst[b], NT, preferred_element_type=jnp.float32)

    def sum_copy(o):
        back = (NZ - ring_order(o, NZ)) % NZ
        slot = ring_slot(back)
        return pltpu.make_async_remote_copy(
            src_ref=wsend.at[o], dst_ref=wrecv.at[slot],
            send_sem=sum_send.at[o], recv_sem=sum_recv.at[slot],
            device_id=at(dz=ring_order(o, NZ)), device_id_type=MESH,
        )

    def ring_slot(away):
        upper = away // (NZ // 2 + 1)
        odd = 2 * away - 1 + (1 - (away + NZ - 1) // NZ)
        return (1 - upper) * odd + upper * 2 * (NZ - away)

    def three(o, carry):
        acc[o] = weigh(0, o) + weigh(1, o) + weigh(2, o)
        return carry

    def finish(n, carry):
        o = NZ - 1 - n
        w = acc[o] + weigh(3, o)
        mass = w[:, E:].T[0:1, :]
        hi = mass.astype(jnp.bfloat16).astype(jnp.float32)
        lo = mass - hi
        rows = jnp.concatenate(
            [hi[:, :E], hi[:, E:], lo[:, :E], lo[:, E:], jnp.zeros((12, E), jnp.float32)], axis=0
        )
        wsend[o, :OWN, :] = w[:, :E].astype(jnp.bfloat16)
        wsend[o, OWN:, :] = rows.astype(jnp.bfloat16)

        @pl.when(o > 0)
        def _():
            sum_copy(o).start()

        return carry

    prepare(0)
    lax.fori_loop(0, 5, first, 0)
    for p in (1, 2):
        key_copy(p).wait_recv()
        core_copy(p).start()
    for p in (1, 2):
        core_copy(p).wait_recv()
    lax.fori_loop(0, 10, near, 0)
    key_copy(3).wait_recv()
    core_copy(3).start()
    lax.fori_loop(0, 9, far, 0)
    for i in range(3):
        send_stats(i)
    core_copy(3).wait_recv()
    lax.fori_loop(0, NZ, last, 0)
    send_stats(3)
    for i in range(3):
        finish_stats(i)
    lax.fori_loop(0, NZ, three, 0)
    finish_stats(3)
    lax.fori_loop(0, NZ, finish, 0)

    for o in range(1, NZ):
        sum_copy(o).wait_recv()
    total = wsend[0].astype(jnp.float32)
    for o in range(1, NZ):
        total = total + wrecv[o].astype(jnp.float32)
    mass = [total[OWN + h : OWN + h + 1] + total[OWN + 2 + h : OWN + 3 + h] for h in range(2)]
    for h in range(2):
        rows = slice(h * E, (h + 1) * E)
        down = jnp.broadcast_to(mass[h], (E, E)).T
        c = code[rows, :].astype(jnp.float32)
        new_code[rows, :] = ((total[rows] + c) / (down + 1.0)).astype(jnp.bfloat16)

    for p in range(1, NX):
        key_copy(p).wait_send()
        core_copy(p).wait_send()
    for o in range(1, NZ):
        code_copy(o).wait_send()
        sum_copy(o).wait_send()
    for i in range(NX):
        all_stats(i).wait_send()


def local(keys, code):
    vmem = pl.BlockSpec(memory_space=pltpu.VMEM)
    bf16, f32 = jnp.bfloat16, jnp.float32
    dma = pltpu.SemaphoreType.DMA
    new_code, loglik = pl.pallas_call(
        kernel,
        out_shape=(
            jax.ShapeDtypeStruct((OWN, E), bf16),
            jax.ShapeDtypeStruct((8, TOK // 8), f32),
        ),
        in_specs=[vmem, vmem],
        out_specs=(vmem, vmem),
        scratch_shapes=[
            pltpu.VMEM((NX, 2 * E, TOK), bf16),
            pltpu.VMEM((NZ, OWN, E), bf16),
            pltpu.VMEM((NZ, OWN, E), bf16),
            pltpu.VMEM((NX * NZ, OWN, TOK), bf16),
            pltpu.VMEM((NX, NZ, TOK), f32),
            pltpu.VMEM((NX, NZ, TOK), f32),
            pltpu.VMEM((NX, NZ, TOK), f32),
            pltpu.VMEM((2, 2 * E, TOK), bf16),
            pltpu.VMEM((NX, 32, 8, TOK // 8), f32),
            pltpu.VMEM((NZ, OWN, 2 * E), f32),
            pltpu.VMEM((NZ, OWN + 16, E), bf16),
            pltpu.VMEM((NZ, OWN + 16, E), bf16),
            dma((NX,)), dma((NX,)), dma((NX,)), dma((NX,)),
            dma((NZ,)), dma((NZ,)), dma((NX,)), dma((NX,)),
            dma((NZ,)), dma((NZ,)),
        ],
        compiler_params=pltpu.CompilerParams(
            collective_id=0, has_side_effects=True, vmem_limit_bytes=48 * 2**20
        ),
    )(keys, code)
    return new_code, loglik.reshape(TOK)


def solution(mesh):
    return jax.shard_map(
        local,
        mesh=mesh,
        in_specs=(P("dp", None), P(("dp", "codebook"), None)),
        out_specs=(P(("dp", "codebook"), None), P("dp")),
        check_vma=False,
    )
```

```python
import jax
import jax.numpy as jnp
from jax import lax
from jax.experimental import pallas as pl
from jax.experimental.pallas import tpu as pltpu
from jax.sharding import PartitionSpec as P

MESH = pl.DeviceIdType.MESH
NX, NZ, NY = 4, 8, 4
TOK, OWN, E = 1024, 256, 128
TILE = 256
HALF = OWN // 2 + 16
BETA = 0.1
LOG2E = 1.4426950408889634
LN2 = 0.6931471805599453
ALPHA = 2.0 * BETA * LOG2E
NT = (((1,), (1,)), ((), ()))
KEY_AT = (0, 1, 3, 2)
KEY_SLOT = (0, 1, 3, 2)
CODE_AT = (0, 1, 7, 2, 6, 3, 5, 4)


def to_tile(row):
    return jnp.concatenate([row[:, 128 * r : 128 * (r + 1)] for r in range(8)], axis=0)


def to_row(tile):
    return jnp.concatenate([tile[r : r + 1, :] for r in range(8)], axis=1)


def kernel(
    keys, code, new_code, loglik,
    raw, kt, cb, prob, top, tot, scale, s0, s1, x0, x1, stats, acc, wsend, wnear, wfar, wrecv,
    in_sem, key_send, key_recv, core_send, core_recv, code_send, code_recv,
    stat_send, stat_recv, sum_send, sum_recv,
):
    dp, col = lax.axis_index("dp"), lax.axis_index("codebook")
    x, z = dp >> 3, dp & 7
    y, core = col >> 1, col & 1
    xs = [((x + d) & 3) << 3 for d in range(NX)]
    zs = [(z + d) & 7 for d in range(NZ)]
    cols = [[(((y + d) & 3) << 1) + ((core + c) & 1) for c in range(2)] for d in range(NY)]

    def at(dx=0, dz=0, dy=0, dc=0):
        return (xs[dx % NX] + zs[dz % NZ], cols[dy % NY][dc % 2])

    others = [(dx, dy, dc) for dx in range(4) for dy in range(4) for dc in range(2)][1:]

    barrier = pltpu.get_barrier_semaphore()
    for dz in range(1, NZ):
        pl.semaphore_signal(barrier, inc=1, device_id=at(dz=dz), device_id_type=MESH)
    for dx, dy, dc in others:
        pl.semaphore_signal(
            barrier, inc=1, device_id=at(dx=dx, dy=dy, dc=dc), device_id_type=MESH
        )

    get_code = pltpu.make_async_copy(code, cb.at[0, :, :E], in_sem.at[0])
    get_keys = pltpu.make_async_copy(keys, raw, in_sem.at[1])
    get_keys.start()
    get_code.start()
    row = lax.broadcasted_iota(jnp.int32, (E, TOK), 0)
    ones = jnp.where(row < 3, 1.0, 0.0).astype(jnp.bfloat16)
    for i in range(NX):
        kt[i, E:, :] = ones
    get_keys.wait()
    kt[0, :E, :] = raw[...].astype(jnp.float32).T.astype(jnp.bfloat16)
    get_code.wait()

    half = pl.ds(pl.multiple_of(core * (E // 2), E // 2), E // 2)

    def remote(src, dst, send, recv, to):
        return pltpu.make_async_remote_copy(
            src_ref=src, dst_ref=dst, send_sem=send, recv_sem=recv,
            device_id=to, device_id_type=MESH,
        )

    def key_copy(p):
        return remote(
            kt.at[0, half], kt.at[p, half], key_send.at[p], key_recv.at[p], at(dx=-KEY_AT[p])
        )

    def core_copy(p):
        return remote(
            kt.at[p, half], kt.at[p, half], core_send.at[p], core_recv.at[p], at(dc=1)
        )

    def code_copy(o):
        return remote(
            cb.at[0, :, :E], cb.at[o, :, :E], code_send.at[o], code_recv.at[o], at(dz=-CODE_AT[o])
        )

    def pass_on(o):
        src, dst, dz = ((3, 5, -1), (4, 6, 1), (3, 7, -2), (4, 7, 2))[o - 5]
        rows = (slice(None), slice(None), slice(0, OWN // 2), slice(OWN // 2, OWN))[o - 5]
        return remote(
            cb.at[src, rows, :E], cb.at[dst, rows, :E], code_send.at[o], code_recv.at[o], at(dz=dz)
        )

    def prepare(o):
        c = cb[o, :, :E].astype(jnp.float32)
        h = -0.5 * jnp.sum(c * c, axis=1, keepdims=True)
        hi = h.astype(jnp.bfloat16).astype(jnp.float32)
        mid = (h - hi).astype(jnp.bfloat16).astype(jnp.float32)
        lo = h - hi - mid
        lane = lax.broadcasted_iota(jnp.int32, (OWN, E), 1)
        both = jnp.where(lane == 0, hi, jnp.where(lane == 1, mid, lo))
        cb[o, :, E:] = jnp.where(lane < 3, both, 0.0).astype(jnp.bfloat16)

    prepare(0)
    pl.semaphore_wait(barrier, len(others) + NZ - 1)
    for p in (1, 2):
        key_copy(p).start()
    for o in (3, 4, 1, 2):
        code_copy(o).start()

    def place(u):
        a = (u + 27) // 32
        b = (u + 22) // 32
        c = (u + 17) // 32
        d = (u + 8) // 32
        near_i = a + b
        near_o = u - 5 * near_i
        t = u - 15
        far_i = t - 3 * (t // 3)
        far_o = 5 + t // 3
        i = (1 - c) * near_i + (c - d) * far_i + 3 * d
        o = (1 - c) * near_o + (c - d) * far_o + d * (u - 24)
        return i, o

    def cross(u, s, m):
        i, o = place(u)
        for q in range(TOK // TILE):
            span = slice(q * TILE, (q + 1) * TILE)
            v = jnp.dot(cb[o], kt[i, :, span], preferred_element_type=jnp.float32)
            s[:, span] = v
            m[:, span] = jnp.max(v.reshape(OWN // 8, 8, TILE), axis=0)
            yield

    def power(u, s, m):
        i, o = place(u)
        k = i * NZ + o
        for q in range(TOK // TILE):
            span = slice(q * TILE, (q + 1) * TILE)
            peak = jnp.max(m[:, span], axis=0, keepdims=True)
            p = jnp.exp2((s[:, span] - peak) * ALPHA)
            top[k, :, span] = jnp.broadcast_to(peak, (8, TILE))
            tot[k, :, span] = jnp.sum(p.reshape(OWN // 8, 8, TILE), axis=0)
            prob[k, :, span] = p.astype(jnp.bfloat16)
            yield

    def both(u, later, now):
        for _ in zip(cross(u + 1, *later), power(u, *now)):
            pass

    def stat_copy(i, r):
        dx, dy, dc = others[r - 1]
        slot = KEY_SLOT[(KEY_AT[i] - dx) % NX]
        return remote(
            stats.at[i, 0], stats.at[slot, r], stat_send.at[i], stat_recv.at[slot],
            at(dx=dx, dy=dy, dc=dc),
        )

    def all_stats(i):
        return remote(
            stats.at[i, pl.ds(1, 31)], stats.at[i, pl.ds(1, 31)],
            stat_send.at[i], stat_recv.at[i], at(dc=1),
        )

    def send_stats(i):
        m = [top[i * NZ + o] for o in range(NZ)]
        peak = m[0]
        for o in range(1, NZ):
            peak = jnp.maximum(peak, m[o])
        total = jnp.zeros_like(peak)
        for o in range(NZ):
            total = total + tot[i * NZ + o] * jnp.exp2((m[o] - peak) * ALPHA)
        total = jnp.sum(total, axis=0, keepdims=True)
        stats[i, 0] = to_tile(ALPHA * peak[0:1] + jnp.log2(total))
        for r in range(1, 32):
            stat_copy(i, r).start()

    def finish_stats(i):
        all_stats(i).wait_recv()
        v = stats[i]
        peak = jnp.max(v, axis=0)
        lse = peak + jnp.log2(jnp.sum(jnp.exp2(v - peak[None]), axis=0))
        if i == 0:
            k = kt[0, :E, :].astype(jnp.float32)
            sq = to_tile(jnp.sum(k * k, axis=0, keepdims=True))
            loglik[...] = LN2 * lse - BETA * sq
        lse = jnp.broadcast_to(to_row(lse), (8, TOK))
        for o in range(NZ):
            f = jnp.exp2(ALPHA * top[i * NZ + o] - lse)
            scale[i * NZ + o] = jnp.concatenate([f, f], axis=0).astype(jnp.bfloat16)

    def on(u, k):
        return pl.when(u == k)

    def ready(u):
        for o in (1, 2, 3, 4):

            @on(u, o)
            def _():
                code_copy(o).wait_recv()
                if o == 3:
                    pass_on(5).start()
                    pass_on(7).start()
                if o == 4:
                    pass_on(6).start()
                    pass_on(8).start()
                prepare(o)

        @on(u, 5)
        def _():
            for p in (1, 2):
                key_copy(p).wait_recv()
                core_copy(p).start()
            key_copy(3).start()
            core_copy(1).wait_recv()

        @on(u, 10)
        def _():
            core_copy(2).wait_recv()

        for o in (5, 6, 7):

            @on(u, 15 + 3 * (o - 5))
            def _():
                if o == 5:
                    key_copy(3).wait_recv()
                    core_copy(3).start()
                pass_on(o).wait_recv()
                if o == 7:
                    pass_on(8).wait_recv()
                prepare(o)

        @on(u, 24)
        def _():
            core_copy(3).wait_recv()

        @on(u, 25)
        def _():
            for i in range(3):
                send_stats(i)

    a, b = (s0, x0), (s1, x1)
    for _ in cross(0, *a):
        pass

    def two(n, carry):
        ready(2 * n + 1)
        both(2 * n, b, a)
        ready(2 * n + 2)
        both(2 * n + 1, a, b)
        return carry

    lax.fori_loop(0, 15, two, 0)
    both(30, b, a)
    for _ in power(31, *b):
        pass
    send_stats(3)

    def weigh(i, o):
        k = i * NZ + o
        p = prob[k].reshape(OWN // 16, 16, TOK) * scale[k][None]
        return lax.dot_general(p.reshape(OWN, TOK), kt[i], NT, preferred_element_type=jnp.float32)

    def three(o, carry):
        acc[o] = weigh(0, o) + weigh(1, o) + weigh(2, o)
        return carry

    for i in range(3):
        finish_stats(i)
    lax.fori_loop(0, NZ, three, 0)
    finish_stats(3)

    def far_copy(o):
        src, dst, dz = (
            (wsend.at[5], wnear.at[0], 1),
            (wsend.at[6], wnear.at[1], -1),
            (wsend.at[7, 0], wfar.at[0], 2),
            (wsend.at[7, 1], wfar.at[1], -2),
        )[o - 5]
        return remote(src, dst, sum_send.at[o], sum_recv.at[o], at(dz=dz))

    def near_copy(o):
        return remote(
            wsend.at[o], wrecv.at[o], sum_send.at[o], sum_recv.at[o], at(dz=CODE_AT[o])
        )

    def finish(n, carry):
        o = NZ - 1 - n
        w = acc[o] + weigh(3, o)
        mass = w[:, E:].T[0:1, :]
        hi = mass.astype(jnp.bfloat16).astype(jnp.float32)
        lo = mass - hi
        for h in range(2):
            rows = slice(h * E, (h + 1) * E)
            wsend[o, h, :E, :] = w[rows, :E].astype(jnp.bfloat16)
            wsend[o, h, E:, :] = jnp.concatenate(
                [hi[:, rows], lo[:, rows], jnp.zeros((14, E), jnp.float32)], axis=0
            ).astype(jnp.bfloat16)

        @on(o, 7)
        def _():
            far_copy(7).start()
            far_copy(8).start()

        for k in (5, 6):

            @on(o, k)
            def _():
                far_copy(k).start()

        for k in (1, 2):

            @on(o, k)
            def _():
                near_copy(k).start()

        return carry

    lax.fori_loop(0, NZ, finish, 0)

    for r in range(2):
        far_copy(5 + r).wait_recv()
        far_copy(7 + r).wait_recv()
        for h in range(2):
            total = wsend[3 + r, h].astype(jnp.float32) + wnear[r, h].astype(jnp.float32)
            if h == r:
                total = total + wfar[r].astype(jnp.float32)
            mass = total[E : E + 1] + total[E + 1 : E + 2]
            hi = mass.astype(jnp.bfloat16).astype(jnp.float32)
            wsend[3 + r, h, :E, :] = total[:E].astype(jnp.bfloat16)
            wsend[3 + r, h, E:, :] = jnp.concatenate(
                [hi, mass - hi, jnp.zeros((14, E), jnp.float32)], axis=0
            ).astype(jnp.bfloat16)
        near_copy(3 + r).start()

    for o in (1, 2, 3, 4):
        near_copy(o).wait_recv()
    for h in range(2):
        total = wsend[0, h].astype(jnp.float32)
        for o in (1, 2, 3, 4):
            total = total + wrecv[o, h].astype(jnp.float32)
        mass = jnp.broadcast_to(total[E : E + 1] + total[E + 1 : E + 2], (E, E)).T
        rows = slice(h * E, (h + 1) * E)
        c = cb[0, rows, :E].astype(jnp.float32)
        new_code[rows, :] = ((total[:E] + c) / (mass + 1.0)).astype(jnp.bfloat16)

    for p in (1, 2, 3):
        key_copy(p).wait_send()
        core_copy(p).wait_send()
    for o in (1, 2, 3, 4):
        code_copy(o).wait_send()
        near_copy(o).wait_send()
    for o in (5, 6, 7, 8):
        pass_on(o).wait_send()
        far_copy(o).wait_send()
    for i in range(NX):
        all_stats(i).wait_send()


def local(keys, code):
    vmem = pl.BlockSpec(memory_space=pltpu.VMEM)
    hbm = pl.BlockSpec(memory_space=pl.ANY)
    bf16, f32 = jnp.bfloat16, jnp.float32
    dma = pltpu.SemaphoreType.DMA
    new_code, loglik = pl.pallas_call(
        kernel,
        out_shape=(
            jax.ShapeDtypeStruct((OWN, E), bf16),
            jax.ShapeDtypeStruct((8, TOK // 8), f32),
        ),
        in_specs=[hbm, hbm],
        out_specs=(vmem, vmem),
        scratch_shapes=[
            pltpu.VMEM((TOK, E), bf16),
            pltpu.VMEM((NX, 2 * E, TOK), bf16),
            pltpu.VMEM((NZ, OWN, 2 * E), bf16),
            pltpu.VMEM((NX * NZ, OWN, TOK), bf16),
            pltpu.VMEM((NX * NZ, 8, TOK), f32),
            pltpu.VMEM((NX * NZ, 8, TOK), f32),
            pltpu.VMEM((NX * NZ, 16, TOK), bf16),
            pltpu.VMEM((OWN, TOK), f32),
            pltpu.VMEM((OWN, TOK), f32),
            pltpu.VMEM((8, TOK), f32),
            pltpu.VMEM((8, TOK), f32),
            pltpu.VMEM((NX, 32, 8, TOK // 8), f32),
            pltpu.VMEM((NZ, OWN, 2 * E), f32),
            pltpu.VMEM((NZ, 2, HALF, E), bf16),
            pltpu.VMEM((2, 2, HALF, E), bf16),
            pltpu.VMEM((2, HALF, E), bf16),
            pltpu.VMEM((5, 2, HALF, E), bf16),
            dma((2,)),
            dma((NX,)), dma((NX,)), dma((NX,)), dma((NX,)),
            dma((NZ + 1,)), dma((NZ + 1,)),
            dma((NX,)), dma((NX,)), dma((NZ + 1,)), dma((NZ + 1,)),
        ],
        compiler_params=pltpu.CompilerParams(
            collective_id=0, has_side_effects=True, vmem_limit_bytes=48 * 2**20
        ),
    )(keys, code)
    return new_code, loglik.reshape(TOK)


def solution(mesh):
    return jax.shard_map(
        local,
        mesh=mesh,
        in_specs=(P("dp", None), P(("dp", "codebook"), None)),
        out_specs=(P(("dp", "codebook"), None), P("dp")),
        check_vma=False,
    )
```

```python
import jax
import jax.numpy as jnp
from jax import lax
from jax.experimental import pallas as pl
from jax.experimental.pallas import tpu as pltpu
from jax.sharding import PartitionSpec as P

MESH = pl.DeviceIdType.MESH
NX, NZ, NY = 4, 8, 4
TOK, OWN, E = 1024, 256, 128
TILE = 256
HALF = OWN // 2 + 16
BETA = 0.1
LOG2E = 1.4426950408889634
LN2 = 0.6931471805599453
ALPHA = 2.0 * BETA * LOG2E
NT = (((1,), (1,)), ((), ()))
CODE_AT = (0, 2, 6, 1, 7, 3, 5, 4)


def to_tile(row):
    return jnp.concatenate([row[:, 128 * r : 128 * (r + 1)] for r in range(8)], axis=0)


def to_row(tile):
    return jnp.concatenate([tile[r : r + 1, :] for r in range(8)], axis=1)


def kernel(
    keys, code, new_code, loglik,
    raw, kt, cb, prob, top, tot, scale, s0, s1, x0, x1, stats, mine, acc, wsend, wnear, wfar, wrecv,
    in_sem, key_send, key_recv, core_send, core_recv, code_send, code_recv,
    stat_send, stat_recv, sum_send, sum_recv,
):
    dp, col = lax.axis_index("dp"), lax.axis_index("codebook")
    x, z = dp >> 3, dp & 7
    y, core = col >> 1, col & 1
    xs = [((x + d) & 3) << 3 for d in range(NX)]
    zs = [(z + d) & 7 for d in range(NZ)]
    cols = [[(((y + d) & 3) << 1) + ((core + c) & 1) for c in range(2)] for d in range(NY)]

    def at(dx=0, dz=0, dy=0, dc=0):
        return (xs[dx % NX] + zs[dz % NZ], cols[dy % NY][dc % 2])

    others = [(dx, dy, dc) for dx in range(4) for dy in range(4) for dc in range(2)][1:]

    barrier = pltpu.get_barrier_semaphore()
    for dz in range(1, NZ):
        pl.semaphore_signal(barrier, inc=1, device_id=at(dz=dz), device_id_type=MESH)
    for dx, dy, dc in others:
        pl.semaphore_signal(
            barrier, inc=1, device_id=at(dx=dx, dy=dy, dc=dc), device_id_type=MESH
        )

    get_code = pltpu.make_async_copy(code, cb.at[0, :, :E], in_sem.at[0])
    get_keys = pltpu.make_async_copy(keys, raw, in_sem.at[1])
    get_keys.start()
    get_code.start()
    row = lax.broadcasted_iota(jnp.int32, (E, TOK), 0)
    ones = jnp.where(row < 3, 1.0, 0.0).astype(jnp.bfloat16)
    for i in range(NX):
        kt[i, E:, :] = ones
    acc[...] = jnp.zeros_like(acc)
    get_keys.wait()
    kt[0, :E, :] = raw[...].astype(jnp.float32).T.astype(jnp.bfloat16)
    get_code.wait()

    def quarter(h):
        return pl.ds(pl.multiple_of(core * (E // 2) + h * (E // 4), E // 4), E // 4)

    half = pl.ds(pl.multiple_of(core * (E // 2), E // 2), E // 2)

    def remote(src, dst, send, recv, to):
        return pltpu.make_async_remote_copy(
            src_ref=src, dst_ref=dst, send_sem=send, recv_sem=recv,
            device_id=to, device_id_type=MESH,
        )

    def key_copy(p, h):
        src = p if p < 3 else 2 - h
        dx = {1: -1, 2: 1}[src]
        return remote(
            kt.at[0 if p < 3 else src, quarter(h)], kt.at[p, quarter(h)],
            key_send.at[2 * p + h], key_recv.at[2 * p + h], at(dx=dx),
        )

    def core_copy(p):
        return remote(
            kt.at[p, half], kt.at[p, half], core_send.at[p], core_recv.at[p], at(dc=1)
        )

    def code_copy(o):
        return remote(
            cb.at[0, :, :E], cb.at[o, :, :E], code_send.at[o], code_recv.at[o], at(dz=-CODE_AT[o])
        )

    def pass_on(o):
        src, dst, dz = ((1, 5, -1), (2, 6, 1), (1, 7, -2), (2, 7, 2))[o - 5]
        rows = (slice(None), slice(None), slice(0, OWN // 2), slice(OWN // 2, OWN))[o - 5]
        return remote(
            cb.at[src, rows, :E], cb.at[dst, rows, :E], code_send.at[o], code_recv.at[o], at(dz=dz)
        )

    def prepare(o):
        c = cb[o, :, :E].astype(jnp.float32)
        h = -0.5 * jnp.sum(c * c, axis=1, keepdims=True)
        hi = h.astype(jnp.bfloat16).astype(jnp.float32)
        mid = (h - hi).astype(jnp.bfloat16).astype(jnp.float32)
        lo = h - hi - mid
        lane = lax.broadcasted_iota(jnp.int32, (OWN, E), 1)
        both = jnp.where(lane == 0, hi, jnp.where(lane == 1, mid, lo))
        cb[o, :, E:] = jnp.where(lane < 3, both, 0.0).astype(jnp.bfloat16)

    prepare(0)
    pl.semaphore_wait(barrier, len(others) + NZ - 1)
    for p, h in ((1, 1), (2, 0), (1, 0), (2, 1)):
        key_copy(p, h).start()
    for o in (1, 2, 3, 4):
        code_copy(o).start()

    def place(u):
        near_i = (u + 27) // 32 + (u + 22) // 32
        near_o = u - 5 * near_i
        far = (u + 17) // 32
        t = u - 15
        opposite = (x + 2) & 3
        t1 = t - 3 * opposite
        t2 = t1 - 8
        b = (t1 + 32) // 32
        c = (t2 + 32) // 32
        n1, n2 = t // 3, t2 // 3
        owner = (1 - b) * n1 + (b - c) * opposite + c * (opposite + 1 + n2)
        away = (owner - x) & 3
        far_i = away + (away >> 1) - 2 * ((away + 1) >> 2)
        far_o = (1 - b) * (5 + t - 3 * n1) + (b - c) * t1 + c * (5 + t2 - 3 * n2)
        return (1 - far) * near_i + far * far_i, (1 - far) * near_o + far * far_o

    def cross(u, s, m):
        i, o = place(u)
        for q in range(TOK // TILE):
            span = slice(q * TILE, (q + 1) * TILE)
            v = jnp.dot(cb[o], kt[i, :, span], preferred_element_type=jnp.float32)
            s[:, span] = v
            m[:, span] = jnp.max(v.reshape(OWN // 8, 8, TILE), axis=0)
            yield

    def power(u, s, m):
        i, o = place(u)
        k = i * NZ + o
        for q in range(TOK // TILE):
            span = slice(q * TILE, (q + 1) * TILE)
            peak = jnp.max(m[:, span], axis=0, keepdims=True)
            p = jnp.exp2((s[:, span] - peak) * ALPHA)
            top[k, :, span] = jnp.broadcast_to(peak, (8, TILE))
            tot[k, :, span] = jnp.sum(p.reshape(OWN // 8, 8, TILE), axis=0)
            prob[k, :, span] = p.astype(jnp.bfloat16)
            yield

    def both(u, later, now):
        for _ in zip(cross(u + 1, *later), power(u, *now)):
            pass

    def all_stats(owner):
        return remote(
            stats.at[owner, pl.ds(1, 31)], stats.at[owner, pl.ds(1, 31)],
            stat_send.at[owner], stat_recv.at[owner], at(dc=1),
        )

    def slot_of(owner):
        away = (owner - x) & 3
        return away + (away >> 1) - 2 * ((away + 1) >> 2)

    def send_stats(owner):
        first = slot_of(owner) * NZ
        m = [top[first + o] for o in range(NZ)]
        peak = m[0]
        for o in range(1, NZ):
            peak = jnp.maximum(peak, m[o])
        total = jnp.zeros_like(peak)
        for o in range(NZ):
            total = total + tot[first + o] * jnp.exp2((m[o] - peak) * ALPHA)
        total = jnp.sum(total, axis=0, keepdims=True)
        stats[owner, 0] = to_tile(ALPHA * peak[0:1] + jnp.log2(total))
        for r, (dx, dy, dc) in enumerate(others):
            remote(
                stats.at[owner, 0], stats.at[owner, r + 1],
                stat_send.at[owner], stat_recv.at[owner], at(dx=dx, dy=dy, dc=dc),
            ).start()

    def finish_stats(owner):
        all_stats(owner).wait_recv()
        first = slot_of(owner) * NZ
        v = stats[owner]
        peak = jnp.max(v, axis=0)
        lse = peak + jnp.log2(jnp.sum(jnp.exp2(v - peak[None]), axis=0))
        mine[owner] = lse
        lse = jnp.broadcast_to(to_row(lse), (8, TOK))
        for o in range(NZ):
            f = jnp.exp2(ALPHA * top[first + o] - lse)
            scale[first + o] = jnp.concatenate([f, f], axis=0).astype(jnp.bfloat16)

    def on(u, k):
        return pl.when(u == k)

    def need_code(o):
        if o < 5:
            code_copy(o).wait_recv()
            if o < 3:
                pass_on(4 + o).start()
                pass_on(6 + o).start()
        else:
            pass_on(o).wait_recv()
        if o == 7:
            pass_on(8).wait_recv()
        prepare(o)

    turn = ((s0, x0), (s1, x1))

    def steps(u, n):
        for j in range(n):
            both(u + j, turn[(j + 1) % 2], turn[j % 2])

    for _ in cross(0, *turn[0]):
        pass
    need_code(1)
    need_code(2)
    for p, h in ((1, 1), (2, 0)):
        key_copy(p, h).wait_recv()
        key_copy(3, h).start()
    for p, h in ((1, 0), (2, 1)):
        key_copy(p, h).wait_recv()
        core_copy(p).start()
    need_code(3)
    need_code(4)

    def near(n, carry):
        for p in (1, 2):
            on(n, p)(lambda p=p: core_copy(p).wait_recv())
        steps(4 * n, 4)
        return carry

    lax.fori_loop(0, 3, near, 0)
    key_copy(3, 0).wait_recv()
    key_copy(3, 1).wait_recv()
    core_copy(3).start()
    steps(12, 2)
    for o in (5, 6, 7):
        need_code(o)
    core_copy(3).wait_recv()

    def done(owner):
        opposite = (x + 2) & 3
        return 17 + 3 * owner + 5 * ((owner - opposite + 4) >> 2)

    def far(n, carry):
        u = 14 + 4 * n
        steps(u, 4)
        for owner in range(3):
            when = (done(owner) - 14) >> 2
            on(n, when)(lambda owner=owner: send_stats(owner))
        return carry

    lax.fori_loop(0, 4, far, 0)
    both(30, turn[1], turn[0])
    for _ in power(31, *turn[1]):
        pass
    send_stats(3)

    def weigh(owner, o, m):
        i = slot_of(owner)
        span = pl.ds(i * NZ + o, m)
        p = prob[span].reshape(m, OWN // 16, 16, TOK) * scale[span][:, None]
        p = p.reshape(m * OWN, TOK)
        w = lax.dot_general(p, kt[i], NT, preferred_element_type=jnp.float32)
        acc[pl.ds(o, m)] += w.reshape(m, OWN, 2 * E)

    def shard(owner, carry):
        finish_stats(owner)
        weigh(owner, 0, NZ)
        return carry

    lax.fori_loop(0, 3, shard, 0)
    finish_stats(3)

    def far_copy(o):
        src, dst, dz = (
            (wsend.at[5], wnear.at[0], 1),
            (wsend.at[6], wnear.at[1], -1),
            (wsend.at[7, 0], wfar.at[0], 2),
            (wsend.at[7, 1], wfar.at[1], -2),
        )[o - 5]
        return remote(src, dst, sum_send.at[o], sum_recv.at[o], at(dz=dz))

    def near_copy(o):
        return remote(
            wsend.at[o], wrecv.at[o], sum_send.at[o], sum_recv.at[o], at(dz=CODE_AT[o])
        )

    def pack(o):
        w = acc[o]
        mass = w[:, E:].T[0:1, :]
        hi = mass.astype(jnp.bfloat16).astype(jnp.float32)
        lo = mass - hi
        for h in range(2):
            rows = slice(h * E, (h + 1) * E)
            wsend[o, h, :E, :] = w[rows, :E].astype(jnp.bfloat16)
            wsend[o, h, E:, :] = jnp.concatenate(
                [hi[:, rows], lo[:, rows], jnp.zeros((14, E), jnp.float32)], axis=0
            ).astype(jnp.bfloat16)

    weigh(3, 4, 4)
    for o in (7, 6, 5, 4):
        pack(o)
        if o == 4:
            near_copy(4).start()
        else:
            far_copy(o).start()
        if o == 7:
            far_copy(8).start()
    weigh(3, 0, 4)
    for o in (3, 2, 1, 0):
        pack(o)
        if o == 3:
            near_copy(3).start()

    k = kt[0, :E, :].astype(jnp.float32)
    sq = to_tile(jnp.sum(k * k, axis=0, keepdims=True))
    loglik[...] = LN2 * mine[x] - BETA * sq

    for r in range(2):
        far_copy(5 + r).wait_recv()
        far_copy(7 + r).wait_recv()
        for h in range(2):
            total = wsend[1 + r, h].astype(jnp.float32) + wnear[r, h].astype(jnp.float32)
            if h == r:
                total = total + wfar[r].astype(jnp.float32)
            mass = total[E : E + 1] + total[E + 1 : E + 2]
            hi = mass.astype(jnp.bfloat16).astype(jnp.float32)
            wsend[1 + r, h, :E, :] = total[:E].astype(jnp.bfloat16)
            wsend[1 + r, h, E:, :] = jnp.concatenate(
                [hi, mass - hi, jnp.zeros((14, E), jnp.float32)], axis=0
            ).astype(jnp.bfloat16)
        near_copy(1 + r).start()

    for o in (1, 2, 3, 4):
        near_copy(o).wait_recv()
    for h in range(2):
        total = wsend[0, h].astype(jnp.float32)
        for o in (1, 2, 3, 4):
            total = total + wrecv[o, h].astype(jnp.float32)
        mass = jnp.broadcast_to(total[E : E + 1] + total[E + 1 : E + 2], (E, E)).T
        rows = slice(h * E, (h + 1) * E)
        c = cb[0, rows, :E].astype(jnp.float32)
        new_code[rows, :] = ((total[:E] + c) / (mass + 1.0)).astype(jnp.bfloat16)

    for p in (1, 2, 3):
        key_copy(p, 0).wait_send()
        key_copy(p, 1).wait_send()
        core_copy(p).wait_send()
    for o in (1, 2, 3, 4):
        code_copy(o).wait_send()
        near_copy(o).wait_send()
    for o in (5, 6, 7, 8):
        pass_on(o).wait_send()
        far_copy(o).wait_send()
    for owner in range(NX):
        all_stats(owner).wait_send()


def local(keys, code):
    vmem = pl.BlockSpec(memory_space=pltpu.VMEM)
    hbm = pl.BlockSpec(memory_space=pl.ANY)
    bf16, f32 = jnp.bfloat16, jnp.float32
    dma = pltpu.SemaphoreType.DMA
    new_code, loglik = pl.pallas_call(
        kernel,
        out_shape=(
            jax.ShapeDtypeStruct((OWN, E), bf16),
            jax.ShapeDtypeStruct((8, TOK // 8), f32),
        ),
        in_specs=[hbm, hbm],
        out_specs=(vmem, vmem),
        scratch_shapes=[
            pltpu.VMEM((TOK, E), bf16),
            pltpu.VMEM((NX, 2 * E, TOK), bf16),
            pltpu.VMEM((NZ, OWN, 2 * E), bf16),
            pltpu.VMEM((NX * NZ, OWN, TOK), bf16),
            pltpu.VMEM((NX * NZ, 8, TOK), f32),
            pltpu.VMEM((NX * NZ, 8, TOK), f32),
            pltpu.VMEM((NX * NZ, 16, TOK), bf16),
            pltpu.VMEM((OWN, TOK), f32),
            pltpu.VMEM((OWN, TOK), f32),
            pltpu.VMEM((8, TOK), f32),
            pltpu.VMEM((8, TOK), f32),
            pltpu.VMEM((NX, 32, 8, TOK // 8), f32),
            pltpu.VMEM((NX, 8, TOK // 8), f32),
            pltpu.VMEM((NZ, OWN, 2 * E), f32),
            pltpu.VMEM((NZ, 2, HALF, E), bf16),
            pltpu.VMEM((2, 2, HALF, E), bf16),
            pltpu.VMEM((2, HALF, E), bf16),
            pltpu.VMEM((5, 2, HALF, E), bf16),
            dma((2,)),
            dma((2 * NX,)), dma((2 * NX,)), dma((NX,)), dma((NX,)),
            dma((NZ + 1,)), dma((NZ + 1,)),
            dma((NX,)), dma((NX,)), dma((NZ + 1,)), dma((NZ + 1,)),
        ],
        compiler_params=pltpu.CompilerParams(
            collective_id=0, has_side_effects=True, vmem_limit_bytes=62 * 2**20
        ),
    )(keys, code)
    return new_code, loglik.reshape(TOK)


def solution(mesh):
    return jax.shard_map(
        local,
        mesh=mesh,
        in_specs=(P("dp", None), P(("dp", "codebook"), None)),
        out_specs=(P(("dp", "codebook"), None), P("dp")),
        check_vma=False,
    )
```

```python
import jax
import jax.numpy as jnp
from jax import lax
from jax.experimental import pallas as pl
from jax.experimental.pallas import tpu as pltpu
from jax.sharding import PartitionSpec as P

MESH = pl.DeviceIdType.MESH
NX, NZ, NY = 4, 8, 4
TOK, OWN, E = 1024, 256, 128
TILE = 256
HALF = OWN // 2 + 16
BETA = 0.1
LOG2E = 1.4426950408889634
LN2 = 0.6931471805599453
ALPHA = 2.0 * BETA * LOG2E
NT = (((1,), (1,)), ((), ()))
CODE_AT = (0, 2, 6, 1, 7, 3, 5, 4)


def to_tile(row):
    return jnp.concatenate([row[:, 128 * r : 128 * (r + 1)] for r in range(8)], axis=0)


def to_row(tile):
    return jnp.concatenate([tile[r : r + 1, :] for r in range(8)], axis=1)


def kernel(
    keys, code, new_code, loglik,
    raw, kt, cb, prob, top, tot, scale, score, high, stats, mine, acc, wsend, wnear, wfar, wrecv,
    in_sem, key_send, key_recv, core_send, core_recv, code_send, code_recv,
    stat_send, stat_recv, sum_send, sum_recv,
):
    dp, col = lax.axis_index("dp"), lax.axis_index("codebook")
    x, z = dp >> 3, dp & 7
    y, core = col >> 1, col & 1
    xs = [((x + d) & 3) << 3 for d in range(NX)]
    zs = [(z + d) & 7 for d in range(NZ)]
    cols = [[(((y + d) & 3) << 1) + ((core + c) & 1) for c in range(2)] for d in range(NY)]

    def at(dx=0, dz=0, dy=0, dc=0):
        return (xs[dx % NX] + zs[dz % NZ], cols[dy % NY][dc % 2])

    others = [(dx, dy, dc) for dx in range(4) for dy in range(4) for dc in range(2)][1:]

    barrier = pltpu.get_barrier_semaphore()
    for dz in range(1, NZ):
        pl.semaphore_signal(barrier, inc=1, device_id=at(dz=dz), device_id_type=MESH)
    for dx, dy, dc in others:
        pl.semaphore_signal(
            barrier, inc=1, device_id=at(dx=dx, dy=dy, dc=dc), device_id_type=MESH
        )

    get_code = pltpu.make_async_copy(code, cb.at[0, :, :E], in_sem.at[0])
    get_keys = pltpu.make_async_copy(keys, raw, in_sem.at[1])
    get_keys.start()
    get_code.start()
    row = lax.broadcasted_iota(jnp.int32, (E, TOK), 0)
    ones = jnp.where(row < 3, 1.0, 0.0).astype(jnp.bfloat16)
    for i in range(NX):
        kt[i, E:, :] = ones
    acc[...] = jnp.zeros_like(acc)
    get_keys.wait()
    kt[0, :E, :] = raw[...].astype(jnp.float32).T.astype(jnp.bfloat16)
    get_code.wait()

    def quarter(h):
        return pl.ds(pl.multiple_of(core * (E // 2) + h * (E // 4), E // 4), E // 4)

    half = pl.ds(pl.multiple_of(core * (E // 2), E // 2), E // 2)

    def remote(src, dst, send, recv, to):
        return pltpu.make_async_remote_copy(
            src_ref=src, dst_ref=dst, send_sem=send, recv_sem=recv,
            device_id=to, device_id_type=MESH,
        )

    def key_copy(p, h):
        src = p if p < 3 else 2 - h
        dx = {1: -1, 2: 1}[src]
        return remote(
            kt.at[0 if p < 3 else src, quarter(h)], kt.at[p, quarter(h)],
            key_send.at[2 * p + h], key_recv.at[2 * p + h], at(dx=dx),
        )

    def core_copy(p):
        return remote(
            kt.at[p, half], kt.at[p, half], core_send.at[p], core_recv.at[p], at(dc=1)
        )

    def code_copy(o):
        return remote(
            cb.at[0, :, :E], cb.at[o, :, :E], code_send.at[o], code_recv.at[o], at(dz=-CODE_AT[o])
        )

    def pass_on(o):
        src, dst, dz = ((1, 5, -1), (2, 6, 1), (1, 7, -2), (2, 7, 2))[o - 5]
        rows = (slice(None), slice(None), slice(0, OWN // 2), slice(OWN // 2, OWN))[o - 5]
        return remote(
            cb.at[src, rows, :E], cb.at[dst, rows, :E], code_send.at[o], code_recv.at[o], at(dz=dz)
        )

    def prepare(o):
        c = cb[o, :, :E].astype(jnp.float32)
        h = -0.5 * jnp.sum(c * c, axis=1, keepdims=True)
        hi = h.astype(jnp.bfloat16).astype(jnp.float32)
        mid = (h - hi).astype(jnp.bfloat16).astype(jnp.float32)
        lo = h - hi - mid
        lane = lax.broadcasted_iota(jnp.int32, (OWN, E), 1)
        both = jnp.where(lane == 0, hi, jnp.where(lane == 1, mid, lo))
        cb[o, :, E:] = jnp.where(lane < 3, both, 0.0).astype(jnp.bfloat16)

    prepare(0)
    pl.semaphore_wait(barrier, len(others) + NZ - 1)
    for p, h in ((1, 1), (2, 0), (1, 0), (2, 1)):
        key_copy(p, h).start()
    for o in (1, 2):
        code_copy(o).start()

    def place(u):
        late = (u + 23) // 32
        v = u - 9 * late
        n3 = v // 3
        near_i = (1 - late) * n3 + late * (v - 3 * n3)
        near_o = (1 - late) * (v - 3 * n3) + late * (3 + n3)
        far = (u + 17) // 32
        t = u - 15
        opposite = (x + 2) & 3
        t1 = t - 3 * opposite
        t2 = t1 - 8
        b = (t1 + 32) // 32
        c = (t2 + 32) // 32
        n1, n2 = t // 3, t2 // 3
        owner = (1 - b) * n1 + (b - c) * opposite + c * (opposite + 1 + n2)
        away = (owner - x) & 3
        far_i = away + (away >> 1) - 2 * ((away + 1) >> 2)
        far_o = (1 - b) * (5 + t - 3 * n1) + (b - c) * t1 + c * (5 + t2 - 3 * n2)
        return (1 - far) * near_i + far * far_i, (1 - far) * near_o + far * far_o

    spans = [slice(q * TILE, (q + 1) * TILE) for q in range(TOK // TILE)]

    def cross(u, span):
        i, o = place(u)
        v = jnp.dot(cb[o], kt[i, :, span], preferred_element_type=jnp.float32)
        score[:, span] = v
        high[:, span] = jnp.max(v.reshape(OWN // 8, 8, TILE), axis=0)

    def power(u, span):
        i, o = place(u)
        k = i * NZ + o
        peak = jnp.max(high[:, span], axis=0, keepdims=True)
        p = jnp.exp2((score[:, span] - peak) * ALPHA)
        top[k, :, span] = jnp.broadcast_to(peak, (8, TILE))
        tot[k, :, span] = jnp.sum(p.reshape(OWN // 8, 8, TILE), axis=0)
        prob[k, :, span] = p.astype(jnp.bfloat16)

    def all_stats(owner):
        return remote(
            stats.at[owner, pl.ds(1, 31)], stats.at[owner, pl.ds(1, 31)],
            stat_send.at[owner], stat_recv.at[owner], at(dc=1),
        )

    def slot_of(owner):
        away = (owner - x) & 3
        return away + (away >> 1) - 2 * ((away + 1) >> 2)

    def send_stats(owner):
        first = slot_of(owner) * NZ
        m = [top[first + o] for o in range(NZ)]
        peak = m[0]
        for o in range(1, NZ):
            peak = jnp.maximum(peak, m[o])
        total = jnp.zeros_like(peak)
        for o in range(NZ):
            total = total + tot[first + o] * jnp.exp2((m[o] - peak) * ALPHA)
        total = jnp.sum(total, axis=0, keepdims=True)
        stats[owner, 0] = to_tile(ALPHA * peak[0:1] + jnp.log2(total))
        for r, (dx, dy, dc) in enumerate(others):
            remote(
                stats.at[owner, 0], stats.at[owner, r + 1],
                stat_send.at[owner], stat_recv.at[owner], at(dx=dx, dy=dy, dc=dc),
            ).start()

    def finish_stats(owner):
        all_stats(owner).wait_recv()
        first = slot_of(owner) * NZ
        v = stats[owner]
        peak = jnp.max(v, axis=0)
        lse = peak + jnp.log2(jnp.sum(jnp.exp2(v - peak[None]), axis=0))
        mine[owner] = lse
        lse = jnp.broadcast_to(to_row(lse), (8, TOK))
        for o in range(NZ):
            f = jnp.exp2(ALPHA * top[first + o] - lse)
            scale[first + o] = jnp.concatenate([f, f], axis=0).astype(jnp.bfloat16)

    def on(u, k):
        return pl.when(u == k)

    def need_code(o):
        if o < 5:
            code_copy(o).wait_recv()
            if o < 3:
                pass_on(4 + o).start()
                pass_on(6 + o).start()
        else:
            pass_on(o).wait_recv()
        if o == 7:
            pass_on(8).wait_recv()
        prepare(o)

    def steps(u, n):
        for j in range(n):
            for span in spans:
                power(u + j, span)
                cross(u + j + 1, span)

    for span in spans:
        cross(0, span)
    for p, h in ((1, 1), (2, 0)):
        key_copy(p, h).wait_recv()
        key_copy(3, h).start()
    for o in (3, 4):
        code_copy(o).start()
    need_code(1)
    need_code(2)
    for p, h in ((1, 0), (2, 1)):
        key_copy(p, h).wait_recv()
        core_copy(p).start()
    steps(0, 2)

    def near(n, carry):
        @on(n, 0)
        def _():
            core_copy(1).wait_recv()
            core_copy(2).wait_recv()

        @on(n, 1)
        def _():
            need_code(3)
            need_code(4)

        @on(n, 2)
        def _():
            key_copy(3, 0).wait_recv()
            key_copy(3, 1).wait_recv()
            core_copy(3).start()

        steps(2 + 4 * n, 4)
        return carry

    lax.fori_loop(0, 3, near, 0)
    for o in (5, 6, 7):
        need_code(o)
    core_copy(3).wait_recv()

    def done(owner):
        opposite = (x + 2) & 3
        return 17 + 3 * owner + 5 * ((owner - opposite + 4) >> 2)

    def far(n, carry):
        u = 14 + 4 * n
        steps(u, 4)
        for owner in range(3):
            when = (done(owner) - 14) >> 2
            on(n, when)(lambda owner=owner: send_stats(owner))
        return carry

    lax.fori_loop(0, 4, far, 0)
    steps(30, 1)
    for span in spans:
        power(31, span)
    send_stats(3)

    def weigh(owner, o, m):
        i = slot_of(owner)
        span = pl.ds(i * NZ + o, m)
        p = prob[span].reshape(m, OWN // 16, 16, TOK) * scale[span][:, None]
        p = p.reshape(m * OWN, TOK)
        w = lax.dot_general(p, kt[i], NT, preferred_element_type=jnp.float32)
        acc[pl.ds(o, m)] += w.reshape(m, OWN, 2 * E)

    def shard(owner, carry):
        finish_stats(owner)
        weigh(owner, 0, NZ)
        return carry

    lax.fori_loop(0, 3, shard, 0)
    finish_stats(3)

    def far_copy(o, h):
        dst, dz = {5: (wnear.at[0, h], 1), 6: (wnear.at[1, h], -1), 7: (wfar.at[h], 2 - 4 * h)}[o]
        k = 2 * o + h
        return remote(wsend.at[o, h], dst, sum_send.at[k], sum_recv.at[k], at(dz=dz))

    def near_copy(o, h):
        k = 2 * o + h
        return remote(
            wsend.at[o, h], wrecv.at[o, h], sum_send.at[k], sum_recv.at[k], at(dz=CODE_AT[o])
        )

    def pack(o):
        w = acc[o]
        mass = w[:, E:].T[0:1, :]
        hi = mass.astype(jnp.bfloat16).astype(jnp.float32)
        lo = mass - hi
        for h in range(2):
            rows = slice(h * E, (h + 1) * E)
            wsend[o, h, :E, :] = w[rows, :E].astype(jnp.bfloat16)
            wsend[o, h, E:, :] = jnp.concatenate(
                [hi[:, rows], lo[:, rows], jnp.zeros((14, E), jnp.float32)], axis=0
            ).astype(jnp.bfloat16)

    weigh(3, 5, 3)
    pack(5)
    pack(6)
    far_copy(5, 1).start()
    far_copy(6, 0).start()
    pack(7)
    for o, h in ((7, 0), (7, 1), (5, 0), (6, 1)):
        far_copy(o, h).start()
    weigh(3, 0, 5)
    for o in (1, 2, 3, 4, 0):
        pack(o)

    k = kt[0, :E, :].astype(jnp.float32)
    sq = to_tile(jnp.sum(k * k, axis=0, keepdims=True))
    loglik[...] = LN2 * mine[x] - BETA * sq

    def relay(r, h):
        far_copy(5 + r, h).wait_recv()
        total = wsend[1 + r, h].astype(jnp.float32) + wnear[r, h].astype(jnp.float32)
        if h == r:
            far_copy(7, h).wait_recv()
            total = total + wfar[r].astype(jnp.float32)
        mass = total[E : E + 1] + total[E + 1 : E + 2]
        hi = mass.astype(jnp.bfloat16).astype(jnp.float32)
        wsend[1 + r, h, :E, :] = total[:E].astype(jnp.bfloat16)
        wsend[1 + r, h, E:, :] = jnp.concatenate(
            [hi, mass - hi, jnp.zeros((14, E), jnp.float32)], axis=0
        ).astype(jnp.bfloat16)
        near_copy(1 + r, h).start()

    relay(0, 1)
    relay(1, 0)
    for o in (3, 4):
        for h in range(2):
            near_copy(o, h).start()
    relay(0, 0)
    relay(1, 1)

    for o in (3, 4, 1, 2):
        for h in range(2):
            near_copy(o, h).wait_recv()
    for h in range(2):
        total = wsend[0, h].astype(jnp.float32)
        for o in (1, 2, 3, 4):
            total = total + wrecv[o, h].astype(jnp.float32)
        mass = jnp.broadcast_to(total[E : E + 1] + total[E + 1 : E + 2], (E, E)).T
        rows = slice(h * E, (h + 1) * E)
        c = cb[0, rows, :E].astype(jnp.float32)
        new_code[rows, :] = ((total[:E] + c) / (mass + 1.0)).astype(jnp.bfloat16)

    for p in (1, 2, 3):
        key_copy(p, 0).wait_send()
        key_copy(p, 1).wait_send()
        core_copy(p).wait_send()
    for o in (1, 2, 3, 4):
        code_copy(o).wait_send()
        near_copy(o, 0).wait_send()
        near_copy(o, 1).wait_send()
    for o in (5, 6, 7, 8):
        pass_on(o).wait_send()
    for o in (5, 6, 7):
        far_copy(o, 0).wait_send()
        far_copy(o, 1).wait_send()
    for owner in range(NX):
        all_stats(owner).wait_send()


def local(keys, code):
    vmem = pl.BlockSpec(memory_space=pltpu.VMEM)
    hbm = pl.BlockSpec(memory_space=pl.ANY)
    bf16, f32 = jnp.bfloat16, jnp.float32
    dma = pltpu.SemaphoreType.DMA
    new_code, loglik = pl.pallas_call(
        kernel,
        out_shape=(
            jax.ShapeDtypeStruct((OWN, E), bf16),
            jax.ShapeDtypeStruct((8, TOK // 8), f32),
        ),
        in_specs=[hbm, hbm],
        out_specs=(vmem, vmem),
        scratch_shapes=[
            pltpu.VMEM((TOK, E), bf16),
            pltpu.VMEM((NX, 2 * E, TOK), bf16),
            pltpu.VMEM((NZ, OWN, 2 * E), bf16),
            pltpu.VMEM((NX * NZ, OWN, TOK), bf16),
            pltpu.VMEM((NX * NZ, 8, TOK), f32),
            pltpu.VMEM((NX * NZ, 8, TOK), f32),
            pltpu.VMEM((NX * NZ, 16, TOK), bf16),
            pltpu.VMEM((OWN, TOK), f32),
            pltpu.VMEM((8, TOK), f32),
            pltpu.VMEM((NX, 32, 8, TOK // 8), f32),
            pltpu.VMEM((NX, 8, TOK // 8), f32),
            pltpu.VMEM((NZ, OWN, 2 * E), f32),
            pltpu.VMEM((NZ, 2, HALF, E), bf16),
            pltpu.VMEM((2, 2, HALF, E), bf16),
            pltpu.VMEM((2, HALF, E), bf16),
            pltpu.VMEM((5, 2, HALF, E), bf16),
            dma((2,)),
            dma((2 * NX,)), dma((2 * NX,)), dma((NX,)), dma((NX,)),
            dma((NZ + 1,)), dma((NZ + 1,)),
            dma((NX,)), dma((NX,)), dma((2 * NZ,)), dma((2 * NZ,)),
        ],
        compiler_params=pltpu.CompilerParams(
            collective_id=0, has_side_effects=True, vmem_limit_bytes=62 * 2**20
        ),
    )(keys, code)
    return new_code, loglik.reshape(TOK)


def solution(mesh):
    return jax.shard_map(
        local,
        mesh=mesh,
        in_specs=(P("dp", None), P(("dp", "codebook"), None)),
        out_specs=(P(("dp", "codebook"), None), P("dp")),
        check_vma=False,
    )
```

```python
import jax
import jax.numpy as jnp
from jax import lax
from jax.experimental import pallas as pl
from jax.experimental.pallas import tpu as pltpu
from jax.sharding import PartitionSpec as P

MESH = pl.DeviceIdType.MESH
NX, NZ, NY = 4, 8, 4
TOK, OWN, E = 1024, 256, 128
TILE = 256
HALF = OWN // 2 + 16
BETA = 0.1
LOG2E = 1.4426950408889634
LN2 = 0.6931471805599453
ALPHA = 2.0 * BETA * LOG2E
NT = (((1,), (1,)), ((), ()))
CODE_AT = (0, 2, 6, 1, 7, 3, 5, 4)


def to_tile(row):
    return jnp.concatenate([row[:, 128 * r : 128 * (r + 1)] for r in range(8)], axis=0)


def to_row(tile):
    return jnp.concatenate([tile[r : r + 1, :] for r in range(8)], axis=1)


def kernel(
    keys, code, new_code, loglik,
    raw, kt, cb, prob, top, tot, scale, score, high, stats, mine, acc, wsend, wnear, wfar, wrecv,
    in_sem, key_send, key_recv, core_send, core_recv, code_send, code_recv,
    stat_send, stat_recv, sum_send, sum_recv, met,
):
    dp, col = lax.axis_index("dp"), lax.axis_index("codebook")
    x, z = dp >> 3, dp & 7
    y, core = col >> 1, col & 1
    xs = [((x + d) & 3) << 3 for d in range(NX)]
    zs = [(z + d) & 7 for d in range(NZ)]
    cols = [[(((y + d) & 3) << 1) + ((core + c) & 1) for c in range(2)] for d in range(NY)]

    def at(dx=0, dz=0, dy=0, dc=0):
        return (xs[dx % NX] + zs[dz % NZ], cols[dy % NY][dc % 2])

    others = [(dx, dy, dc) for dx in range(4) for dy in range(4) for dc in range(2)][1:]

    column = [(dy, dc) for dy in range(4) for dc in range(2)][1:]
    close = [at(dz=d) for d in (2, -2, 1, -1)] + [at(dx=d) for d in (2, 1, -1)]
    close += [at(dy=dy, dc=dc) for dy, dc in column]
    barrier = pltpu.get_barrier_semaphore()
    for to in close:
        pl.semaphore_signal(barrier, inc=1, device_id=to, device_id_type=MESH)

    get_code = pltpu.make_async_copy(code, cb.at[0, :, :E], in_sem.at[0])
    get_keys = pltpu.make_async_copy(keys, raw, in_sem.at[1])
    get_keys.start()
    get_code.start()
    for i in range(NX):
        kt[i, E:, :] = jnp.ones((E, TOK), jnp.bfloat16)
    acc[...] = jnp.zeros_like(acc)
    get_keys.wait()
    kt[0, :E, :] = raw[...].astype(jnp.float32).T.astype(jnp.bfloat16)
    get_code.wait()

    def quarter(h):
        return pl.ds(pl.multiple_of(core * (E // 2) + h * (E // 4), E // 4), E // 4)

    half = pl.ds(pl.multiple_of(core * (E // 2), E // 2), E // 2)

    def remote(src, dst, send, recv, to):
        return pltpu.make_async_remote_copy(
            src_ref=src, dst_ref=dst, send_sem=send, recv_sem=recv,
            device_id=to, device_id_type=MESH,
        )

    def key_copy(p, h):
        src = p if p < 3 else 2 - h
        dx = {1: -1, 2: 1}[src]
        return remote(
            kt.at[0 if p < 3 else src, quarter(h)], kt.at[p, quarter(h)],
            key_send.at[2 * p + h], key_recv.at[2 * p + h], at(dx=dx),
        )

    def core_copy(p):
        return remote(
            kt.at[p, half], kt.at[p, half], core_send.at[p], core_recv.at[p], at(dc=1)
        )

    def code_copy(o):
        return remote(
            cb.at[0, :, :E], cb.at[o, :, :E], code_send.at[o], code_recv.at[o], at(dz=-CODE_AT[o])
        )

    def pass_on(o):
        src, dst, dz = ((1, 5, -1), (2, 6, 1), (1, 7, -2), (2, 7, 2))[o - 5]
        rows = (slice(None), slice(None), slice(0, OWN // 2), slice(OWN // 2, OWN))[o - 5]
        return remote(
            cb.at[src, rows, :E], cb.at[dst, rows, :E], code_send.at[o], code_recv.at[o], at(dz=dz)
        )

    def prepare(o):
        c = cb[o, :, :E].astype(jnp.float32)
        h = -0.5 * jnp.sum(c * c, axis=1, keepdims=True)
        hi = h.astype(jnp.bfloat16).astype(jnp.float32)
        mid = (h - hi).astype(jnp.bfloat16).astype(jnp.float32)
        lo = h - hi - mid
        lane = lax.broadcasted_iota(jnp.int32, (OWN, E), 1)
        both = jnp.where(lane == 0, hi, jnp.where(lane == 1, mid, lo))
        cb[o, :, E:] = jnp.where(lane < 3, both, 0.0).astype(jnp.bfloat16)

    prepare(0)
    pl.semaphore_wait(barrier, len(close))
    for p, h in ((1, 1), (2, 0), (1, 0), (2, 1)):
        key_copy(p, h).start()
    for o in (1, 2):
        code_copy(o).start()

    def place(u):
        late = (u + 23) // 32
        v = u - 9 * late
        n3 = v // 3
        near_i = (1 - late) * n3 + late * (v - 3 * n3)
        near_o = (1 - late) * (v - 3 * n3) + late * (3 + n3)
        far = (u + 17) // 32
        t = u - 15
        opposite = (x + 2) & 3
        t1 = t - 3 * opposite
        t2 = t1 - 8
        b = (t1 + 32) // 32
        c = (t2 + 32) // 32
        n1, n2 = t // 3, t2 // 3
        owner = (1 - b) * n1 + (b - c) * opposite + c * (opposite + 1 + n2)
        away = (owner - x) & 3
        far_i = away + (away >> 1) - 2 * ((away + 1) >> 2)
        far_o = (1 - b) * (5 + t - 3 * n1) + (b - c) * t1 + c * (5 + t2 - 3 * n2)
        return (1 - far) * near_i + far * far_i, (1 - far) * near_o + far * far_o

    spans = [slice(q * TILE, (q + 1) * TILE) for q in range(TOK // TILE)]

    def cross(u, span):
        i, o = place(u)
        v = jnp.dot(cb[o], kt[i, :, span], preferred_element_type=jnp.float32)
        score[:, span] = v
        high[:, span] = jnp.max(v.reshape(OWN // 8, 8, TILE), axis=0)

    def power(u, span):
        i, o = place(u)
        k = i * NZ + o
        peak = jnp.max(high[:, span], axis=0, keepdims=True)
        p = jnp.exp2((score[:, span] - peak) * ALPHA)
        top[k, :, span] = jnp.broadcast_to(peak, (8, TILE))
        tot[k, :, span] = jnp.sum(p.reshape(OWN // 8, 8, TILE), axis=0)
        prob[k, :, span] = p.astype(jnp.bfloat16)

    def all_stats(owner):
        return remote(
            stats.at[owner, pl.ds(1, 31)], stats.at[owner, pl.ds(1, 31)],
            stat_send.at[owner], stat_recv.at[owner], at(dc=1),
        )

    def slot_of(owner):
        away = (owner - x) & 3
        return away + (away >> 1) - 2 * ((away + 1) >> 2)

    def send_stats(owner):
        first = slot_of(owner) * NZ
        m = [top[first + o] for o in range(NZ)]
        peak = m[0]
        for o in range(1, NZ):
            peak = jnp.maximum(peak, m[o])
        total = jnp.zeros_like(peak)
        for o in range(NZ):
            total = total + tot[first + o] * jnp.exp2((m[o] - peak) * ALPHA)
        total = jnp.sum(total, axis=0, keepdims=True)
        stats[owner, 0] = to_tile(ALPHA * peak[0:1] + jnp.log2(total))
        for r, (dx, dy, dc) in enumerate(others):
            remote(
                stats.at[owner, 0], stats.at[owner, r + 1],
                stat_send.at[owner], stat_recv.at[owner], at(dx=dx, dy=dy, dc=dc),
            ).start()

    def finish_stats(owner):
        all_stats(owner).wait_recv()
        first = slot_of(owner) * NZ
        v = stats[owner]
        peak = jnp.max(v, axis=0)
        lse = peak + jnp.log2(jnp.sum(jnp.exp2(v - peak[None]), axis=0))
        mine[owner] = lse
        lse = jnp.broadcast_to(to_row(lse), (8, TOK))
        for o in range(NZ):
            f = jnp.exp2(ALPHA * top[first + o] - lse)
            scale[first + o] = jnp.concatenate([f, f], axis=0).astype(jnp.bfloat16)

    def on(u, k):
        return pl.when(u == k)

    def need_code(o):
        if o < 5:
            code_copy(o).wait_recv()
            if o < 3:
                pass_on(4 + o).start()
                pass_on(6 + o).start()
        else:
            pass_on(o).wait_recv()
        if o == 7:
            pass_on(8).wait_recv()
        prepare(o)

    def steps(u, n):
        for j in range(n):
            for span in spans:
                power(u + j, span)
                cross(u + j + 1, span)

    for span in spans:
        cross(0, span)
    for dx in (2, 1, -1):
        pl.semaphore_signal(met, inc=1, device_id=at(dx=dx), device_id_type=MESH)
    for p, h in ((1, 1), (2, 0)):
        key_copy(p, h).wait_recv()
        key_copy(3, h).start()
    for o in (3, 4):
        code_copy(o).start()
    need_code(1)
    need_code(2)
    for p, h in ((1, 0), (2, 1)):
        key_copy(p, h).wait_recv()
        core_copy(p).start()
    steps(0, 2)

    def near(n, carry):
        @on(n, 0)
        def _():
            core_copy(1).wait_recv()
            core_copy(2).wait_recv()

        @on(n, 1)
        def _():
            need_code(3)
            need_code(4)

        @on(n, 2)
        def _():
            key_copy(3, 0).wait_recv()
            key_copy(3, 1).wait_recv()
            core_copy(3).start()

        steps(2 + 4 * n, 4)
        return carry

    lax.fori_loop(0, 3, near, 0)
    for o in (5, 6, 7):
        need_code(o)
    core_copy(3).wait_recv()

    pl.semaphore_wait(met, 3)

    def far(n, carry):
        steps(14 + 4 * n, 4)
        return carry

    lax.fori_loop(0, 2, far, 0)
    steps(22, 1)
    send_stats(0)
    steps(23, 3)
    send_stats(1)
    steps(26, 3)
    send_stats(2)
    steps(29, 2)
    for span in spans:
        power(31, span)
    send_stats(3)

    def weigh(owner, o, m):
        i = slot_of(owner)
        span = pl.ds(i * NZ + o, m)
        p = prob[span].reshape(m, OWN // 16, 16, TOK) * scale[span][:, None]
        p = p.reshape(m * OWN, TOK)
        w = lax.dot_general(p, kt[i], NT, preferred_element_type=jnp.float32)
        acc[pl.ds(o, m)] += w.reshape(m, OWN, 2 * E)

    def shard(owner, carry):
        finish_stats(owner)
        weigh(owner, 0, NZ)
        return carry

    lax.fori_loop(0, 3, shard, 0)
    finish_stats(3)

    def far_copy(o, h):
        dst, dz = {5: (wnear.at[0, h], 1), 6: (wnear.at[1, h], -1), 7: (wfar.at[h], 2 - 4 * h)}[o]
        k = 2 * o + h
        return remote(wsend.at[o, h], dst, sum_send.at[k], sum_recv.at[k], at(dz=dz))

    def near_copy(o, h):
        k = 2 * o + h
        return remote(
            wsend.at[o, h], wrecv.at[o, h], sum_send.at[k], sum_recv.at[k], at(dz=CODE_AT[o])
        )

    diagonal = lax.broadcasted_iota(jnp.int32, (E, E), 0) == lax.broadcasted_iota(
        jnp.int32, (E, E), 1
    )

    def pack(o):
        w = acc[o]
        for h in range(2):
            rows = slice(h * E, (h + 1) * E)
            wsend[o, h, :E, :] = w[rows, :E].astype(jnp.bfloat16)
            mass = jnp.sum(jnp.where(diagonal, w[rows, E:], 0.0), axis=0, keepdims=True)
            hi = mass.astype(jnp.bfloat16).astype(jnp.float32)
            wsend[o, h, E:, :] = jnp.concatenate(
                [hi, mass - hi, jnp.zeros((14, E), jnp.float32)], axis=0
            ).astype(jnp.bfloat16)

    weigh(3, 5, 3)
    pack(5)
    pack(6)
    far_copy(5, 1).start()
    far_copy(6, 0).start()
    pack(7)
    for o, h in ((7, 0), (7, 1), (5, 0), (6, 1)):
        far_copy(o, h).start()
    weigh(3, 0, 5)
    for o in (1, 2, 3, 4, 0):
        pack(o)

    k = kt[0, :E, :].astype(jnp.float32)
    sq = to_tile(jnp.sum(k * k, axis=0, keepdims=True))
    loglik[...] = LN2 * mine[x] - BETA * sq

    def relay(r, h):
        far_copy(5 + r, h).wait_recv()
        total = wsend[1 + r, h].astype(jnp.float32) + wnear[r, h].astype(jnp.float32)
        if h == r:
            far_copy(7, h).wait_recv()
            total = total + wfar[r].astype(jnp.float32)
        mass = total[E : E + 1] + total[E + 1 : E + 2]
        hi = mass.astype(jnp.bfloat16).astype(jnp.float32)
        wsend[1 + r, h, :E, :] = total[:E].astype(jnp.bfloat16)
        wsend[1 + r, h, E:, :] = jnp.concatenate(
            [hi, mass - hi, jnp.zeros((14, E), jnp.float32)], axis=0
        ).astype(jnp.bfloat16)
        near_copy(1 + r, h).start()

    relay(0, 1)
    relay(1, 0)
    for o in (3, 4):
        for h in range(2):
            near_copy(o, h).start()
    relay(0, 0)
    relay(1, 1)

    for o in (3, 4, 1, 2):
        for h in range(2):
            near_copy(o, h).wait_recv()
    for h in range(2):
        total = wsend[0, h].astype(jnp.float32)
        for o in (1, 2, 3, 4):
            total = total + wrecv[o, h].astype(jnp.float32)
        mass = jnp.broadcast_to(total[E : E + 1] + total[E + 1 : E + 2], (E, E)).T
        rows = slice(h * E, (h + 1) * E)
        c = cb[0, rows, :E].astype(jnp.float32)
        new_code[rows, :] = ((total[:E] + c) / (mass + 1.0)).astype(jnp.bfloat16)

    for p in (1, 2, 3):
        key_copy(p, 0).wait_send()
        key_copy(p, 1).wait_send()
        core_copy(p).wait_send()
    for o in (1, 2, 3, 4):
        code_copy(o).wait_send()
        near_copy(o, 0).wait_send()
        near_copy(o, 1).wait_send()
    for o in (5, 6, 7, 8):
        pass_on(o).wait_send()
    for o in (5, 6, 7):
        far_copy(o, 0).wait_send()
        far_copy(o, 1).wait_send()
    for owner in range(NX):
        all_stats(owner).wait_send()


def local(keys, code):
    vmem = pl.BlockSpec(memory_space=pltpu.VMEM)
    hbm = pl.BlockSpec(memory_space=pl.ANY)
    bf16, f32 = jnp.bfloat16, jnp.float32
    dma = pltpu.SemaphoreType.DMA
    new_code, loglik = pl.pallas_call(
        kernel,
        out_shape=(
            jax.ShapeDtypeStruct((OWN, E), bf16),
            jax.ShapeDtypeStruct((8, TOK // 8), f32),
        ),
        in_specs=[hbm, hbm],
        out_specs=(vmem, vmem),
        scratch_shapes=[
            pltpu.VMEM((TOK, E), bf16),
            pltpu.VMEM((NX, 2 * E, TOK), bf16),
            pltpu.VMEM((NZ, OWN, 2 * E), bf16),
            pltpu.VMEM((NX * NZ, OWN, TOK), bf16),
            pltpu.VMEM((NX * NZ, 8, TOK), f32),
            pltpu.VMEM((NX * NZ, 8, TOK), f32),
            pltpu.VMEM((NX * NZ, 16, TOK), bf16),
            pltpu.VMEM((OWN, TOK), f32),
            pltpu.VMEM((8, TOK), f32),
            pltpu.VMEM((NX, 32, 8, TOK // 8), f32),
            pltpu.VMEM((NX, 8, TOK // 8), f32),
            pltpu.VMEM((NZ, OWN, 2 * E), f32),
            pltpu.VMEM((NZ, 2, HALF, E), bf16),
            pltpu.VMEM((2, 2, HALF, E), bf16),
            pltpu.VMEM((2, HALF, E), bf16),
            pltpu.VMEM((5, 2, HALF, E), bf16),
            dma((2,)),
            dma((2 * NX,)), dma((2 * NX,)), dma((NX,)), dma((NX,)),
            dma((NZ + 1,)), dma((NZ + 1,)),
            dma((NX,)), dma((NX,)), dma((2 * NZ,)), dma((2 * NZ,)),
            pltpu.SemaphoreType.REGULAR,
        ],
        compiler_params=pltpu.CompilerParams(
            collective_id=0, has_side_effects=True, vmem_limit_bytes=62 * 2**20
        ),
    )(keys, code)
    return new_code, loglik.reshape(TOK)


def solution(mesh):
    return jax.shard_map(
        local,
        mesh=mesh,
        in_specs=(P("dp", None), P(("dp", "codebook"), None)),
        out_specs=(P(("dp", "codebook"), None), P("dp")),
        check_vma=False,
    )
```

```python
import jax
import jax.numpy as jnp
from jax import lax
from jax.experimental import pallas as pl
from jax.experimental.pallas import tpu as pltpu
from jax.sharding import PartitionSpec as P

MESH = pl.DeviceIdType.MESH
NX, NZ, NY = 4, 8, 4
TOK, OWN, E = 1024, 256, 128
TILE = 256
HALF = OWN // 2 + 16
BETA = 0.1
LOG2E = 1.4426950408889634
LN2 = 0.6931471805599453
ALPHA = 2.0 * BETA * LOG2E
NT = (((1,), (1,)), ((), ()))
CODE_AT = (0, 2, 6, 1, 7, 3, 5, 4)


def to_tile(row):
    return jnp.concatenate([row[:, 128 * r : 128 * (r + 1)] for r in range(8)], axis=0)


def to_row(tile):
    return jnp.concatenate([tile[r : r + 1, :] for r in range(8)], axis=1)


def kernel(
    keys, code, new_code, loglik,
    raw, kt, cb, prob, top, tot, scale, score, high, stats, mine, acc, wsend, wnear, wfar, wrecv,
    in_sem, key_send, key_recv, core_send, core_recv, code_send, code_recv,
    stat_send, stat_recv, sum_send, sum_recv, met,
):
    dp, col = lax.axis_index("dp"), lax.axis_index("codebook")
    x, z = dp >> 3, dp & 7
    y, core = col >> 1, col & 1
    xs = [((x + d) & 3) << 3 for d in range(NX)]
    zs = [(z + d) & 7 for d in range(NZ)]
    cols = [[(((y + d) & 3) << 1) + ((core + c) & 1) for c in range(2)] for d in range(NY)]

    def at(dx=0, dz=0, dy=0, dc=0):
        return (xs[dx % NX] + zs[dz % NZ], cols[dy % NY][dc % 2])

    others = [(dx, dy, dc) for dx in range(4) for dy in range(4) for dc in range(2)][1:]

    get_code = pltpu.make_async_copy(code, cb.at[0, :, :E], in_sem.at[0])
    get_keys = pltpu.make_async_copy(keys, raw, in_sem.at[1])
    get_keys.start()
    get_code.start()

    column = [(dy, dc) for dy in range(4) for dc in range(2)][1:]
    close = [at(dz=d) for d in (2, -2, 1, -1)] + [at(dx=d) for d in (2, 1, -1)]
    close += [at(dy=dy, dc=dc) for dy, dc in column]
    barrier = pltpu.get_barrier_semaphore()
    for to in close:
        pl.semaphore_signal(barrier, inc=1, device_id=to, device_id_type=MESH)

    get_keys.wait()
    kt[0, :E, :] = raw[...].astype(jnp.float32).T.astype(jnp.bfloat16)
    get_code.wait()

    def quarter(h):
        return pl.ds(pl.multiple_of(core * (E // 2) + h * (E // 4), E // 4), E // 4)

    def remote(src, dst, send, recv, to):
        return pltpu.make_async_remote_copy(
            src_ref=src, dst_ref=dst, send_sem=send, recv_sem=recv,
            device_id=to, device_id_type=MESH,
        )

    def key_copy(p, h):
        src = p if p < 3 else 2 - h
        dx = {1: -1, 2: 1}[src]
        return remote(
            kt.at[0 if p < 3 else src, quarter(h)], kt.at[p, quarter(h)],
            key_send.at[2 * p + h], key_recv.at[2 * p + h], at(dx=dx),
        )

    def core_copy(p, h):
        k = 2 * p + h
        return remote(
            kt.at[p, quarter(h)], kt.at[p, quarter(h)], core_send.at[k], core_recv.at[k], at(dc=1)
        )

    def code_copy(o):
        return remote(
            cb.at[0, :, :E], cb.at[o, :, :E], code_send.at[o], code_recv.at[o], at(dz=-CODE_AT[o])
        )

    def pass_on(o):
        src, dst, dz = ((1, 5, -1), (2, 6, 1), (1, 7, -2), (2, 7, 2))[o - 5]
        rows = (slice(None), slice(None), slice(0, OWN // 2), slice(OWN // 2, OWN))[o - 5]
        return remote(
            cb.at[src, rows, :E], cb.at[dst, rows, :E], code_send.at[o], code_recv.at[o], at(dz=dz)
        )

    def prepare(o):
        c = cb[o, :, :E].astype(jnp.float32)
        h = -0.5 * jnp.sum(c * c, axis=1, keepdims=True)
        hi = h.astype(jnp.bfloat16).astype(jnp.float32)
        mid = (h - hi).astype(jnp.bfloat16).astype(jnp.float32)
        lo = h - hi - mid
        lane = lax.broadcasted_iota(jnp.int32, (OWN, E), 1)
        both = jnp.where(lane == 0, hi, jnp.where(lane == 1, mid, lo))
        cb[o, :, E:] = jnp.where(lane < 3, both, 0.0).astype(jnp.bfloat16)

    pl.semaphore_wait(barrier, len(close))
    for p, h in ((1, 1), (2, 0), (1, 0), (2, 1)):
        key_copy(p, h).start()
    for o in (1, 2):
        code_copy(o).start()
    for dx in (2, 1, -1):
        pl.semaphore_signal(met, inc=1, device_id=at(dx=dx), device_id_type=MESH)
    for i in range(NX):
        kt[i, E:, :] = jnp.ones((E, TOK), jnp.bfloat16)
    acc[...] = jnp.zeros_like(acc)
    prepare(0)

    def place(u):
        late = (u + 23) // 32
        v = u - 9 * late
        n3 = v // 3
        near_i = (1 - late) * n3 + late * (v - 3 * n3)
        near_o = (1 - late) * (v - 3 * n3) + late * (3 + n3)
        far = (u + 17) // 32
        t = u - 15
        opposite = (x + 2) & 3
        t1 = t - 3 * opposite
        t2 = t1 - 8
        b = (t1 + 32) // 32
        c = (t2 + 32) // 32
        n1, n2 = t // 3, t2 // 3
        owner = (1 - b) * n1 + (b - c) * opposite + c * (opposite + 1 + n2)
        away = (owner - x) & 3
        far_i = away + (away >> 1) - 2 * ((away + 1) >> 2)
        far_o = (1 - b) * (5 + t - 3 * n1) + (b - c) * t1 + c * (5 + t2 - 3 * n2)
        return (1 - far) * near_i + far * far_i, (1 - far) * near_o + far * far_o

    spans = [slice(q * TILE, (q + 1) * TILE) for q in range(TOK // TILE)]

    def cross(u, span):
        i, o = place(u)
        v = jnp.dot(cb[o], kt[i, :, span], preferred_element_type=jnp.float32)
        score[:, span] = v
        high[:, span] = jnp.max(v.reshape(OWN // 8, 8, TILE), axis=0)

    def power(u, span):
        i, o = place(u)
        k = i * NZ + o
        peak = jnp.max(high[:, span], axis=0, keepdims=True)
        p = jnp.exp2((score[:, span] - peak) * ALPHA)
        top[k, :, span] = jnp.broadcast_to(peak, (8, TILE))
        tot[k, :, span] = jnp.sum(p.reshape(OWN // 8, 8, TILE), axis=0)
        prob[k, :, span] = p.astype(jnp.bfloat16)

    def all_stats(owner):
        return remote(
            stats.at[owner, pl.ds(1, 31)], stats.at[owner, pl.ds(1, 31)],
            stat_send.at[owner], stat_recv.at[owner], at(dc=1),
        )

    def slot_of(owner):
        away = (owner - x) & 3
        return away + (away >> 1) - 2 * ((away + 1) >> 2)

    def send_stats(owner):
        first = slot_of(owner) * NZ
        m = [top[first + o] for o in range(NZ)]
        peak = m[0]
        for o in range(1, NZ):
            peak = jnp.maximum(peak, m[o])
        total = jnp.zeros_like(peak)
        for o in range(NZ):
            total = total + tot[first + o] * jnp.exp2((m[o] - peak) * ALPHA)
        total = jnp.sum(total, axis=0, keepdims=True)
        stats[owner, 0] = to_tile(ALPHA * peak[0:1] + jnp.log2(total))
        for r, (dx, dy, dc) in enumerate(others):
            remote(
                stats.at[owner, 0], stats.at[owner, r + 1],
                stat_send.at[owner], stat_recv.at[owner], at(dx=dx, dy=dy, dc=dc),
            ).start()

    def finish_stats(owner):
        all_stats(owner).wait_recv()
        first = slot_of(owner) * NZ
        v = stats[owner]
        peak = jnp.max(v, axis=0)
        lse = peak + jnp.log2(jnp.sum(jnp.exp2(v - peak[None]), axis=0))
        mine[owner] = lse
        lse = jnp.broadcast_to(to_row(lse), (8, TOK))
        for o in range(NZ):
            f = jnp.exp2(ALPHA * top[first + o] - lse)
            scale[first + o] = jnp.concatenate([f, f], axis=0).astype(jnp.bfloat16)

    def on(u, k):
        return pl.when(u == k)

    def need_code(o):
        if o < 5:
            code_copy(o).wait_recv()
            if o < 3:
                pass_on(4 + o).start()
                pass_on(6 + o).start()
        else:
            pass_on(o).wait_recv()
        if o == 7:
            pass_on(8).wait_recv()
        prepare(o)

    def steps(u, n):
        for j in range(n):
            for span in spans:
                power(u + j, span)
                cross(u + j + 1, span)

    for span in spans:
        cross(0, span)
    for p, h in ((1, 1), (2, 0)):
        key_copy(p, h).wait_recv()
        key_copy(3, h).start()
        core_copy(p, h).start()
    for o in (3, 4):
        code_copy(o).start()
    need_code(1)
    need_code(2)
    for p, h in ((1, 0), (2, 1)):
        key_copy(p, h).wait_recv()
        core_copy(p, h).start()
    steps(0, 2)

    def near(n, carry):
        @on(n, 0)
        def _():
            for p in (1, 2):
                core_copy(p, 0).wait_recv()
                core_copy(p, 1).wait_recv()

        @on(n, 1)
        def _():
            need_code(3)
            need_code(4)

        @on(n, 2)
        def _():
            for h in range(2):
                key_copy(3, h).wait_recv()
                core_copy(3, h).start()

        steps(2 + 4 * n, 4)
        return carry

    lax.fori_loop(0, 3, near, 0)
    need_code(5)
    need_code(6)
    core_copy(3, 0).wait_recv()
    core_copy(3, 1).wait_recv()
    need_code(7)
    pl.semaphore_wait(met, 3)

    def far(n, carry):
        steps(14 + 4 * n, 4)
        return carry

    lax.fori_loop(0, 2, far, 0)
    steps(22, 1)
    send_stats(0)
    steps(23, 4)
    send_stats(1)
    steps(27, 4)
    send_stats(2)
    for span in spans:
        power(31, span)
    send_stats(3)

    def weigh(owner, o, m):
        i = slot_of(owner)
        span = pl.ds(i * NZ + o, m)
        p = prob[span].reshape(m, OWN // 16, 16, TOK) * scale[span][:, None]
        p = p.reshape(m * OWN, TOK)
        w = lax.dot_general(p, kt[i], NT, preferred_element_type=jnp.float32)
        acc[pl.ds(o, m)] += w.reshape(m, OWN, 2 * E)

    def shard(owner, carry):
        finish_stats(owner)
        weigh(owner, 0, NZ)
        return carry

    lax.fori_loop(0, 3, shard, 0)
    finish_stats(3)

    def far_copy(o, h):
        dst, dz = {5: (wnear.at[0, h], 1), 6: (wnear.at[1, h], -1), 7: (wfar.at[h], 2 - 4 * h)}[o]
        k = 2 * o + h
        return remote(wsend.at[o, h], dst, sum_send.at[k], sum_recv.at[k], at(dz=dz))

    def near_copy(o, h):
        k = 2 * o + h
        return remote(
            wsend.at[o, h], wrecv.at[o, h], sum_send.at[k], sum_recv.at[k], at(dz=CODE_AT[o])
        )

    diagonal = lax.broadcasted_iota(jnp.int32, (E, E), 0) == lax.broadcasted_iota(
        jnp.int32, (E, E), 1
    )

    def pack(o):
        w = acc[o]
        for h in range(2):
            rows = slice(h * E, (h + 1) * E)
            wsend[o, h, :E, :] = w[rows, :E].astype(jnp.bfloat16)
            mass = jnp.sum(jnp.where(diagonal, w[rows, E:], 0.0), axis=0, keepdims=True)
            hi = mass.astype(jnp.bfloat16).astype(jnp.float32)
            wsend[o, h, E:, :] = jnp.concatenate(
                [hi, mass - hi, jnp.zeros((14, E), jnp.float32)], axis=0
            ).astype(jnp.bfloat16)

    weigh(3, 5, 3)
    pack(5)
    pack(6)
    far_copy(5, 1).start()
    far_copy(6, 0).start()
    pack(7)
    for o, h in ((7, 0), (7, 1), (5, 0), (6, 1)):
        far_copy(o, h).start()
    weigh(3, 0, 5)
    for o in (1, 2, 3, 4, 0):
        pack(o)

    k = kt[0, :E, :].astype(jnp.float32)
    sq = to_tile(jnp.sum(k * k, axis=0, keepdims=True))
    loglik[...] = LN2 * mine[x] - BETA * sq

    def relay(r, h):
        far_copy(5 + r, h).wait_recv()
        total = wsend[1 + r, h].astype(jnp.float32) + wnear[r, h].astype(jnp.float32)
        if h == r:
            far_copy(7, h).wait_recv()
            total = total + wfar[r].astype(jnp.float32)
        mass = total[E : E + 1] + total[E + 1 : E + 2]
        hi = mass.astype(jnp.bfloat16).astype(jnp.float32)
        wsend[1 + r, h, :E, :] = total[:E].astype(jnp.bfloat16)
        wsend[1 + r, h, E:, :] = jnp.concatenate(
            [hi, mass - hi, jnp.zeros((14, E), jnp.float32)], axis=0
        ).astype(jnp.bfloat16)
        near_copy(1 + r, h).start()

    relay(0, 1)
    relay(1, 0)
    for o in (3, 4):
        for h in range(2):
            near_copy(o, h).start()
    relay(0, 0)
    relay(1, 1)

    for o in (3, 4, 1, 2):
        for h in range(2):
            near_copy(o, h).wait_recv()
    for h in range(2):
        total = wsend[0, h].astype(jnp.float32)
        for o in (1, 2, 3, 4):
            total = total + wrecv[o, h].astype(jnp.float32)
        mass = jnp.broadcast_to(total[E : E + 1] + total[E + 1 : E + 2], (E, E)).T
        rows = slice(h * E, (h + 1) * E)
        c = cb[0, rows, :E].astype(jnp.float32)
        new_code[rows, :] = ((total[:E] + c) / (mass + 1.0)).astype(jnp.bfloat16)

    for p in (1, 2, 3):
        key_copy(p, 0).wait_send()
        key_copy(p, 1).wait_send()
        core_copy(p, 0).wait_send()
        core_copy(p, 1).wait_send()
    for o in (1, 2, 3, 4):
        code_copy(o).wait_send()
        near_copy(o, 0).wait_send()
        near_copy(o, 1).wait_send()
    for o in (5, 6, 7, 8):
        pass_on(o).wait_send()
    for o in (5, 6, 7):
        far_copy(o, 0).wait_send()
        far_copy(o, 1).wait_send()
    for owner in range(NX):
        all_stats(owner).wait_send()


def local(keys, code):
    vmem = pl.BlockSpec(memory_space=pltpu.VMEM)
    hbm = pl.BlockSpec(memory_space=pl.ANY)
    bf16, f32 = jnp.bfloat16, jnp.float32
    dma = pltpu.SemaphoreType.DMA
    new_code, loglik = pl.pallas_call(
        kernel,
        out_shape=(
            jax.ShapeDtypeStruct((OWN, E), bf16),
            jax.ShapeDtypeStruct((8, TOK // 8), f32),
        ),
        in_specs=[hbm, hbm],
        out_specs=(vmem, vmem),
        scratch_shapes=[
            pltpu.VMEM((TOK, E), bf16),
            pltpu.VMEM((NX, 2 * E, TOK), bf16),
            pltpu.VMEM((NZ, OWN, 2 * E), bf16),
            pltpu.VMEM((NX * NZ, OWN, TOK), bf16),
            pltpu.VMEM((NX * NZ, 8, TOK), f32),
            pltpu.VMEM((NX * NZ, 8, TOK), f32),
            pltpu.VMEM((NX * NZ, 16, TOK), bf16),
            pltpu.VMEM((OWN, TOK), f32),
            pltpu.VMEM((8, TOK), f32),
            pltpu.VMEM((NX, 32, 8, TOK // 8), f32),
            pltpu.VMEM((NX, 8, TOK // 8), f32),
            pltpu.VMEM((NZ, OWN, 2 * E), f32),
            pltpu.VMEM((NZ, 2, HALF, E), bf16),
            pltpu.VMEM((2, 2, HALF, E), bf16),
            pltpu.VMEM((2, HALF, E), bf16),
            pltpu.VMEM((5, 2, HALF, E), bf16),
            dma((2,)),
            dma((2 * NX,)), dma((2 * NX,)), dma((2 * NX,)), dma((2 * NX,)),
            dma((NZ + 1,)), dma((NZ + 1,)),
            dma((NX,)), dma((NX,)), dma((2 * NZ,)), dma((2 * NZ,)),
            pltpu.SemaphoreType.REGULAR,
        ],
        compiler_params=pltpu.CompilerParams(
            collective_id=0, has_side_effects=True, vmem_limit_bytes=62 * 2**20
        ),
    )(keys, code)
    return new_code, loglik.reshape(TOK)


def solution(mesh):
    return jax.shard_map(
        local,
        mesh=mesh,
        in_specs=(P("dp", None), P(("dp", "codebook"), None)),
        out_specs=(P(("dp", "codebook"), None), P("dp")),
        check_vma=False,
    )
```

```python
import jax
import jax.numpy as jnp
from jax import lax
from jax.experimental import pallas as pl
from jax.experimental.pallas import tpu as pltpu
from jax.sharding import PartitionSpec as P

MESH = pl.DeviceIdType.MESH
NX, NZ, NY = 4, 8, 4
TOK, OWN, E = 1024, 256, 128
TILE = 256
HALF = OWN // 2 + 16
BETA = 0.1
LOG2E = 1.4426950408889634
LN2 = 0.6931471805599453
ALPHA = 2.0 * BETA * LOG2E
NT = (((1,), (1,)), ((), ()))
CODE_AT = (0, 2, 6, 1, 7, 3, 5, 4)


def to_tile(row):
    return jnp.concatenate([row[:, 128 * r : 128 * (r + 1)] for r in range(8)], axis=0)


def to_row(tile):
    return jnp.concatenate([tile[r : r + 1, :] for r in range(8)], axis=1)


def kernel(
    keys, code, new_code, loglik,
    raw, kt, cb, prob, top, tot, scale, score, high, stats, mine, acc, wsend, wnear, wfar, wrecv,
    in_sem, key_send, key_recv, core_send, core_recv, code_send, code_recv,
    stat_send, stat_recv, sum_send, sum_recv, met,
):
    dp, col = lax.axis_index("dp"), lax.axis_index("codebook")
    x, z = dp >> 3, dp & 7
    y, core = col >> 1, col & 1
    xs = [((x + d) & 3) << 3 for d in range(NX)]
    zs = [(z + d) & 7 for d in range(NZ)]
    cols = [[(((y + d) & 3) << 1) + ((core + c) & 1) for c in range(2)] for d in range(NY)]

    def at(dx=0, dz=0, dy=0, dc=0):
        return (xs[dx % NX] + zs[dz % NZ], cols[dy % NY][dc % 2])

    others = [(dx, dy, dc) for dx in range(4) for dy in range(4) for dc in range(2)][1:]

    get_code = pltpu.make_async_copy(code, cb.at[0, :, :E], in_sem.at[0])
    get_keys = pltpu.make_async_copy(keys, raw, in_sem.at[1])
    get_keys.start()
    get_code.start()

    column = [(dy, dc) for dy in range(4) for dc in range(2)][1:]
    close = [at(dz=d) for d in (2, -2, 1, -1)] + [at(dx=d) for d in (2, 1, -1)]
    close += [at(dy=dy, dc=dc) for dy, dc in column]
    barrier = pltpu.get_barrier_semaphore()
    for to in close:
        pl.semaphore_signal(barrier, inc=1, device_id=to, device_id_type=MESH)

    get_keys.wait()
    kt[0, :E, :] = raw[...].astype(jnp.float32).T.astype(jnp.bfloat16)
    get_code.wait()

    def quarter(h):
        return pl.ds(pl.multiple_of(core * (E // 2) + h * (E // 4), E // 4), E // 4)

    def remote(src, dst, send, recv, to):
        return pltpu.make_async_remote_copy(
            src_ref=src, dst_ref=dst, send_sem=send, recv_sem=recv,
            device_id=to, device_id_type=MESH,
        )

    def key_copy(p, h):
        src = p if p < 3 else 2 - h
        dx = {1: -1, 2: 1}[src]
        return remote(
            kt.at[0 if p < 3 else src, quarter(h)], kt.at[p, quarter(h)],
            key_send.at[2 * p + h], key_recv.at[2 * p + h], at(dx=dx),
        )

    def core_copy(p, h):
        k = 2 * p + h
        return remote(
            kt.at[p, quarter(h)], kt.at[p, quarter(h)], core_send.at[k], core_recv.at[k], at(dc=1)
        )

    def code_copy(o):
        return remote(
            cb.at[0, :, :E], cb.at[o, :, :E], code_send.at[o], code_recv.at[o], at(dz=-CODE_AT[o])
        )

    def pass_on(o):
        src, dst, dz = ((1, 5, -1), (2, 6, 1), (1, 7, -2), (2, 7, 2))[o - 5]
        rows = (slice(None), slice(None), slice(0, OWN // 2), slice(OWN // 2, OWN))[o - 5]
        return remote(
            cb.at[src, rows, :E], cb.at[dst, rows, :E], code_send.at[o], code_recv.at[o], at(dz=dz)
        )

    def prepare(o):
        c = cb[o, :, :E].astype(jnp.float32)
        h = -0.5 * jnp.sum(c * c, axis=1, keepdims=True)
        hi = h.astype(jnp.bfloat16).astype(jnp.float32)
        mid = (h - hi).astype(jnp.bfloat16).astype(jnp.float32)
        lo = h - hi - mid
        lane = lax.broadcasted_iota(jnp.int32, (OWN, E), 1)
        both = jnp.where(lane == 0, hi, jnp.where(lane == 1, mid, lo))
        cb[o, :, E:] = jnp.where(lane < 3, both, 0.0).astype(jnp.bfloat16)

    pl.semaphore_wait(barrier, len(close))
    for p, h in ((1, 1), (2, 0), (1, 0), (2, 1)):
        key_copy(p, h).start()
    for o in (1, 2):
        code_copy(o).start()
    for dx in (2, 1, -1):
        pl.semaphore_signal(met, inc=1, device_id=at(dx=dx), device_id_type=MESH)
    for i in range(NX):
        kt[i, E:, :] = jnp.ones((E, TOK), jnp.bfloat16)
    acc[...] = jnp.zeros_like(acc)
    prepare(0)

    def place(u):
        late = (u + 23) // 32
        v = u - 9 * late
        n3 = v // 3
        near_i = (1 - late) * n3 + late * (v - 3 * n3)
        near_o = (1 - late) * (v - 3 * n3) + late * (3 + n3)
        far = (u + 17) // 32
        t = u - 15
        opposite = (x + 2) & 3
        t1 = t - 3 * opposite
        t2 = t1 - 8
        b = (t1 + 32) // 32
        c = (t2 + 32) // 32
        n1, n2 = t // 3, t2 // 3
        owner = (1 - b) * n1 + (b - c) * opposite + c * (opposite + 1 + n2)
        away = (owner - x) & 3
        far_i = away + (away >> 1) - 2 * ((away + 1) >> 2)
        far_o = (1 - b) * (5 + t - 3 * n1) + (b - c) * t1 + c * (5 + t2 - 3 * n2)
        return (1 - far) * near_i + far * far_i, (1 - far) * near_o + far * far_o

    spans = [slice(q * TILE, (q + 1) * TILE) for q in range(TOK // TILE)]

    def cross(u, span):
        i, o = place(u)
        v = jnp.dot(cb[o], kt[i, :, span], preferred_element_type=jnp.float32)
        score[:, span] = v
        high[:, span] = jnp.max(v.reshape(OWN // 8, 8, TILE), axis=0)

    def power(u, span):
        i, o = place(u)
        k = i * NZ + o
        peak = jnp.max(high[:, span], axis=0, keepdims=True)
        p = jnp.exp2((score[:, span] - peak) * ALPHA)
        top[k, :, span] = jnp.broadcast_to(peak, (8, TILE))
        tot[k, :, span] = jnp.sum(p.reshape(OWN // 8, 8, TILE), axis=0)
        prob[k, :, span] = p.astype(jnp.bfloat16)

    def all_stats(owner):
        return remote(
            stats.at[owner, pl.ds(1, 31)], stats.at[owner, pl.ds(1, 31)],
            stat_send.at[owner], stat_recv.at[owner], at(dc=1),
        )

    def slot_of(owner):
        away = (owner - x) & 3
        return away + (away >> 1) - 2 * ((away + 1) >> 2)

    def send_stats(owner):
        first = slot_of(owner) * NZ
        m = [top[first + o] for o in range(NZ)]
        peak = m[0]
        for o in range(1, NZ):
            peak = jnp.maximum(peak, m[o])
        total = jnp.zeros_like(peak)
        for o in range(NZ):
            total = total + tot[first + o] * jnp.exp2((m[o] - peak) * ALPHA)
        total = jnp.sum(total, axis=0, keepdims=True)
        stats[owner, 0] = to_tile(ALPHA * peak[0:1] + jnp.log2(total))
        for r, (dx, dy, dc) in enumerate(others):
            remote(
                stats.at[owner, 0], stats.at[owner, r + 1],
                stat_send.at[owner], stat_recv.at[owner], at(dx=dx, dy=dy, dc=dc),
            ).start()

    def finish_stats(owner):
        all_stats(owner).wait_recv()
        first = slot_of(owner) * NZ
        v = stats[owner]
        peak = jnp.max(v, axis=0)
        lse = peak + jnp.log2(jnp.sum(jnp.exp2(v - peak[None]), axis=0))
        mine[owner] = lse
        lse = jnp.broadcast_to(to_row(lse), (8, TOK))
        for o in range(NZ):
            f = jnp.exp2(ALPHA * top[first + o] - lse)
            scale[first + o] = jnp.concatenate([f, f], axis=0).astype(jnp.bfloat16)

    def on(u, k):
        return pl.when(u == k)

    def need_code(o):
        if o < 5:
            code_copy(o).wait_recv()
            if o < 3:
                pass_on(4 + o).start()
                pass_on(6 + o).start()
        else:
            pass_on(o).wait_recv()
        if o == 7:
            pass_on(8).wait_recv()
        prepare(o)

    def steps(u, n):
        for j in range(n):
            for span in spans:
                power(u + j, span)
                cross(u + j + 1, span)

    for span in spans:
        cross(0, span)
    for p, h in ((1, 1), (2, 0)):
        key_copy(p, h).wait_recv()
        key_copy(3, h).start()
        core_copy(p, h).start()
    for o in (3, 4):
        code_copy(o).start()
    need_code(1)
    need_code(2)
    for p, h in ((1, 0), (2, 1)):
        key_copy(p, h).wait_recv()
        core_copy(p, h).start()
    steps(0, 2)

    def near(n, carry):
        @on(n, 0)
        def _():
            for p in (1, 2):
                core_copy(p, 0).wait_recv()
                core_copy(p, 1).wait_recv()

        @on(n, 1)
        def _():
            need_code(3)
            need_code(4)

        @on(n, 2)
        def _():
            for h in range(2):
                key_copy(3, h).wait_recv()
                core_copy(3, h).start()

        steps(2 + 4 * n, 4)
        return carry

    lax.fori_loop(0, 3, near, 0)
    need_code(5)
    need_code(6)
    core_copy(3, 0).wait_recv()
    core_copy(3, 1).wait_recv()
    need_code(7)
    pl.semaphore_wait(met, 3)

    def far(n, carry):
        steps(14 + 4 * n, 4)
        return carry

    lax.fori_loop(0, 2, far, 0)
    steps(22, 1)
    send_stats(0)
    steps(23, 4)
    send_stats(1)
    steps(27, 4)
    send_stats(2)
    for span in spans:
        power(31, span)
    send_stats(3)

    def weigh(owner, o, m):
        i = slot_of(owner)
        span = pl.ds(i * NZ + o, m)
        p = prob[span].reshape(m, OWN // 16, 16, TOK) * scale[span][:, None]
        p = p.reshape(m * OWN, TOK)
        w = lax.dot_general(p, kt[i], NT, preferred_element_type=jnp.float32)
        acc[pl.ds(o, m)] += w.reshape(m, OWN, 2 * E)

    def shard(owner, carry):
        finish_stats(owner)
        weigh(owner, 0, NZ)
        return carry

    lax.fori_loop(0, 3, shard, 0)
    finish_stats(3)

    def far_copy(o, h):
        dst, dz = {5: (wnear.at[0, h], 1), 6: (wnear.at[1, h], -1), 7: (wfar.at[h], 2 - 4 * h)}[o]
        k = 2 * o + h
        return remote(wsend.at[o, h], dst, sum_send.at[k], sum_recv.at[k], at(dz=dz))

    def near_copy(o, h):
        k = 2 * o + h
        return remote(
            wsend.at[o, h], wrecv.at[o, h], sum_send.at[k], sum_recv.at[k], at(dz=CODE_AT[o])
        )

    diagonal = lax.broadcasted_iota(jnp.int32, (E, E), 0) == lax.broadcasted_iota(
        jnp.int32, (E, E), 1
    )

    def pack(o):
        w = acc[o]
        for h in range(2):
            rows = slice(h * E, (h + 1) * E)
            wsend[o, h, :E, :] = w[rows, :E].astype(jnp.bfloat16)
            mass = jnp.sum(jnp.where(diagonal, w[rows, E:], 0.0), axis=0, keepdims=True)
            hi = mass.astype(jnp.bfloat16).astype(jnp.float32)
            wsend[o, h, E:, :] = jnp.concatenate(
                [hi, mass - hi, jnp.zeros((14, E), jnp.float32)], axis=0
            ).astype(jnp.bfloat16)

    weigh(3, 5, 3)
    pack(7)
    far_copy(7, 0).start()
    far_copy(7, 1).start()
    pack(5)
    pack(6)
    for o, h in ((5, 1), (6, 0), (5, 0), (6, 1)):
        far_copy(o, h).start()
    weigh(3, 0, 5)
    for o in (1, 2, 3, 4, 0):
        pack(o)

    k = kt[0, :E, :].astype(jnp.float32)
    sq = to_tile(jnp.sum(k * k, axis=0, keepdims=True))
    loglik[...] = LN2 * mine[x] - BETA * sq

    def relay(r, h):
        far_copy(5 + r, h).wait_recv()
        total = wsend[1 + r, h].astype(jnp.float32) + wnear[r, h].astype(jnp.float32)
        if h == r:
            far_copy(7, h).wait_recv()
            total = total + wfar[r].astype(jnp.float32)
        mass = total[E : E + 1] + total[E + 1 : E + 2]
        hi = mass.astype(jnp.bfloat16).astype(jnp.float32)
        wsend[1 + r, h, :E, :] = total[:E].astype(jnp.bfloat16)
        wsend[1 + r, h, E:, :] = jnp.concatenate(
            [hi, mass - hi, jnp.zeros((14, E), jnp.float32)], axis=0
        ).astype(jnp.bfloat16)
        near_copy(1 + r, h).start()

    relay(0, 1)
    relay(1, 0)
    for o in (3, 4):
        for h in range(2):
            near_copy(o, h).start()
    relay(0, 0)
    relay(1, 1)

    for o in (3, 4, 1, 2):
        for h in range(2):
            near_copy(o, h).wait_recv()
    for h in range(2):
        total = wsend[0, h].astype(jnp.float32)
        for o in (1, 2, 3, 4):
            total = total + wrecv[o, h].astype(jnp.float32)
        mass = jnp.broadcast_to(total[E : E + 1] + total[E + 1 : E + 2], (E, E)).T
        rows = slice(h * E, (h + 1) * E)
        c = cb[0, rows, :E].astype(jnp.float32)
        new_code[rows, :] = ((total[:E] + c) / (mass + 1.0)).astype(jnp.bfloat16)

    for p in (1, 2, 3):
        key_copy(p, 0).wait_send()
        key_copy(p, 1).wait_send()
        core_copy(p, 0).wait_send()
        core_copy(p, 1).wait_send()
    for o in (1, 2, 3, 4):
        code_copy(o).wait_send()
        near_copy(o, 0).wait_send()
        near_copy(o, 1).wait_send()
    for o in (5, 6, 7, 8):
        pass_on(o).wait_send()
    for o in (5, 6, 7):
        far_copy(o, 0).wait_send()
        far_copy(o, 1).wait_send()
    for owner in range(NX):
        all_stats(owner).wait_send()


def local(keys, code):
    vmem = pl.BlockSpec(memory_space=pltpu.VMEM)
    hbm = pl.BlockSpec(memory_space=pl.ANY)
    bf16, f32 = jnp.bfloat16, jnp.float32
    dma = pltpu.SemaphoreType.DMA
    new_code, loglik = pl.pallas_call(
        kernel,
        out_shape=(
            jax.ShapeDtypeStruct((OWN, E), bf16),
            jax.ShapeDtypeStruct((8, TOK // 8), f32),
        ),
        in_specs=[hbm, hbm],
        out_specs=(vmem, vmem),
        scratch_shapes=[
            pltpu.VMEM((TOK, E), bf16),
            pltpu.VMEM((NX, 2 * E, TOK), bf16),
            pltpu.VMEM((NZ, OWN, 2 * E), bf16),
            pltpu.VMEM((NX * NZ, OWN, TOK), bf16),
            pltpu.VMEM((NX * NZ, 8, TOK), f32),
            pltpu.VMEM((NX * NZ, 8, TOK), f32),
            pltpu.VMEM((NX * NZ, 16, TOK), bf16),
            pltpu.VMEM((OWN, TOK), f32),
            pltpu.VMEM((8, TOK), f32),
            pltpu.VMEM((NX, 32, 8, TOK // 8), f32),
            pltpu.VMEM((NX, 8, TOK // 8), f32),
            pltpu.VMEM((NZ, OWN, 2 * E), f32),
            pltpu.VMEM((NZ, 2, HALF, E), bf16),
            pltpu.VMEM((2, 2, HALF, E), bf16),
            pltpu.VMEM((2, HALF, E), bf16),
            pltpu.VMEM((5, 2, HALF, E), bf16),
            dma((2,)),
            dma((2 * NX,)), dma((2 * NX,)), dma((2 * NX,)), dma((2 * NX,)),
            dma((NZ + 1,)), dma((NZ + 1,)),
            dma((NX,)), dma((NX,)), dma((2 * NZ,)), dma((2 * NZ,)),
            pltpu.SemaphoreType.REGULAR,
        ],
        compiler_params=pltpu.CompilerParams(
            collective_id=0, has_side_effects=True, vmem_limit_bytes=62 * 2**20
        ),
    )(keys, code)
    return new_code, loglik.reshape(TOK)


def solution(mesh):
    return jax.shard_map(
        local,
        mesh=mesh,
        in_specs=(P("dp", None), P(("dp", "codebook"), None)),
        out_specs=(P(("dp", "codebook"), None), P("dp")),
        check_vma=False,
    )
```
